32 devices in a mesh: light: 4 (over z), view: 8 (over y, x, core).
Axes of the slice: x: 2, y: 2, z: 4, core: 2. Of those that a mesh axis runs over, the one named last changes fastest.
Arguments:
- density: bfloat16 [1024, 64, 512], P('view', None, 'light'), may hold values from 0 to 8, as said below
- color_coef: float32 [3, 4], replicated, may hold values from 0.2 to 1
Outputs:
- image: float32 [3, 64, 512], P(None, 'view', 'light')
The draws below stay inside these ranges and needn't reach their ends.
Inputs may be any that keep to these rules, and one draw needn't show every extreme that they name: `density`: densities are nonnegative.
All inputs are finite; a program needn't handle non-finite values.
Results may differ from the reference program's by a relative error of at most 0.0003.
Values sent between devices are 32-bit elements; how exact they have to be, the bound alone decides.
No kernel may reach another device: no remote copies, remote signals or barrier semaphores. Data moves between devices by JAX's collectives and lax.ppermute only.
A program may use at most 64 MiB of HBM per device.

```python
import math
import jax
import jax.numpy as jnp
from jax import lax

CV = 128
CL = 128
Z = 64
NV = 1024
NL = 512


def draw_density(key, part):
    view_tile = max(CV // 2, 1)
    key_rough, key_level = jax.random.split(key, 2)
    rough_part = jax.random.uniform(key_rough, (NV, Z, NL), jnp.float32, 0.0, 1.0)
    level_grid = jnp.exp(jax.random.uniform(key_level, (NV // view_tile, Z, NL // CL), jnp.float32, math.log(0.25), math.log(4.0)))
    level_grid = jnp.repeat(jnp.repeat(level_grid, view_tile, axis=0), CL, axis=2)
    return (rough_part * level_grid).astype(jnp.bfloat16)


def setup_inputs(seed: int = 0) -> dict:
    streams_of = jax.random.split(jax.random.key(seed), 3)
    density = draw_density(jax.random.fold_in(streams_of[2], 71), 0)
    color_coef = jnp.clip(jax.random.uniform(streams_of[1], (3, 4), jnp.float32, 0.2, 1.0), 0.2, 1.0)
    return {"density": density, "color_coef": color_coef}


def reference(density, color_coef):
    total_view = density.shape[0]
    block_rows = math.gcd(total_view, 128)
    blocks = density.reshape(total_view // block_rows, block_rows, Z, NL)

    def advance(carry, block):
        depth_sheet, picture = carry
        values = block.astype(jnp.float32)
        light_step = (2.0 / NL) * values
        lit = jnp.exp(-(jnp.cumsum(light_step, axis=2) - light_step))
        view_step = (2.0 / NV) * values
        view_depth = depth_sheet[None] + jnp.cumsum(view_step, axis=0) - view_step
        alpha = 1.0 - jnp.exp(-view_step)
        weight = alpha * (0.3 + lit) * jnp.exp(-view_depth)
        coef = color_coef[:, :, None, None, None]
        palette = coef[:, 0] + values[None] * (coef[:, 1] + values[None] * (coef[:, 2] + values[None] * coef[:, 3]))
        picture = picture + jnp.sum(palette * weight[None], axis=1)
        depth_sheet = depth_sheet + jnp.sum(view_step, axis=0)
        return (depth_sheet, picture), None

    start = (jnp.zeros((Z, NL), jnp.float32), jnp.zeros((3, Z, NL), jnp.float32))
    (depth_sheet, picture), unused = lax.scan(advance, start, blocks)
    return picture
```

```python
import functools
import math

import jax
import jax.numpy as jnp
from jax import lax
from jax.experimental import pallas as pl
from jax.experimental.pallas import tpu as pltpu
from jax.sharding import PartitionSpec as P

VMEM = pltpu.VMEM
LOG2E = math.log2(math.e)
STEP = 8


def swapped(x, axis, mask):
    devices = lax.axis_size(axis)
    return lax.ppermute(x, axis, [(i, i ^ mask) for i in range(devices)])


def paired(x, rows):
    half = x.shape[0] // 2
    lanes = x.shape[-1]
    return jnp.concatenate(
        [x[:half].reshape(half * rows, lanes), x[half:].reshape(half * rows, lanes)], axis=1
    )


def unpaired(y, rows):
    lanes = y.shape[1] // 2
    return jnp.concatenate(
        [y[:, :lanes].reshape(-1, rows, lanes), y[:, lanes:].reshape(-1, rows, lanes)], axis=0
    )


def twice(square):
    zero = jnp.zeros_like(square)
    return jnp.concatenate(
        [jnp.concatenate([square, zero], axis=1), jnp.concatenate([zero, square], axis=1)], axis=0
    )


def totals_kernel(chunk, density_ref, totals_ref, brick_ref, sem):
    cells, planes, lanes = brick_ref.shape
    copies = []
    for k in range(cells // chunk):
        at = pl.ds(k * chunk, chunk)
        copies.append(pltpu.make_async_copy(density_ref.at[at], brick_ref.at[at], sem.at[k]))
        copies[-1].start()
    ones = twice(jnp.ones((lanes, lanes), jnp.bfloat16))
    lane = lax.broadcasted_iota(jnp.int32, (planes, cells), 1)
    total = jnp.zeros((planes, cells), jnp.float32)
    for k in range(cells // chunk):
        copies[k].wait()

        def step(s, total, k=k):
            first = k * chunk + s * STEP
            sums = unpaired(
                jnp.dot(
                    paired(brick_ref[pl.ds(first, STEP)], planes),
                    ones,
                    preferred_element_type=jnp.float32,
                ),
                planes,
            )
            for j in range(STEP):
                total = jnp.where(lane == first + j, sums[j], total)
            return total

        total = lax.fori_loop(0, chunk // STEP, step, total)
    totals_ref[...] = total


def local_kernel(rows, light_scale, view_scale, brick_ref, shade_ref, still_ref):
    cells, planes, lanes = brick_ref.shape
    before = lax.broadcasted_iota(jnp.int32, (lanes, lanes), 0)
    after = lax.broadcasted_iota(jnp.int32, (lanes, lanes), 1)
    earlier = twice((before < after).astype(jnp.bfloat16))
    for z in range(0, planes, rows):
        at = pl.ds(z, rows)

        def step(s, state, at=at):
            through, m1, m2, m3 = state
            first = s * STEP
            packed = brick_ref[pl.ds(first, STEP), at]
            run = unpaired(
                jnp.dot(paired(packed, rows), earlier, preferred_element_type=jnp.float32), rows
            )
            for j in range(STEP):
                value = packed[j].astype(jnp.float32)
                after = through * jnp.exp2(value * view_scale)
                weight = through - after
                through = after
                shade_ref[first + j, at] = weight * jnp.exp2(run[j] * light_scale)
                weight = weight * value
                m1 = m1 + weight
                weight = weight * value
                m2 = m2 + weight
                weight = weight * value
                m3 = m3 + weight
            return through, m1, m2, m3

        zero = jnp.zeros((rows, lanes), jnp.float32)
        through, m1, m2, m3 = lax.fori_loop(
            0, cells // STEP, step, (jnp.ones((rows, lanes), jnp.float32), zero, zero, zero)
        )
        still_ref[0, at] = through
        still_ref[1, at] = m1
        still_ref[2, at] = m2
        still_ref[3, at] = m3


def lit_kernel(rows, light_scale, coef_ref, brick_ref, shade_ref, still_ref, upstream_ref, out_ref):
    cells, planes, lanes = brick_ref.shape
    for z in range(0, planes, rows):
        at = pl.ds(z, rows)
        reach = jnp.exp2(upstream_ref[at] * light_scale)

        def step(s, state, at=at):
            reach, m0, m1, m2, m3 = state
            first = s * STEP
            packed = brick_ref[pl.ds(first, STEP), at]
            for j in range(STEP):
                value = packed[j].astype(jnp.float32)
                weight = shade_ref[first + j, at] * reach[:, j : j + 1]
                m0 = m0 + weight
                weight = weight * value
                m1 = m1 + weight
                weight = weight * value
                m2 = m2 + weight
                weight = weight * value
                m3 = m3 + weight
            return pltpu.roll(reach, cells - STEP, 1), m0, m1, m2, m3

        zero = jnp.zeros((rows, lanes), jnp.float32)
        _, m0, m1, m2, m3 = lax.fori_loop(0, cells // STEP, step, (reach, zero, zero, zero, zero))
        through = still_ref[0, at]
        m0 = m0 + 0.3 * (1.0 - through)
        m1 = m1 + 0.3 * still_ref[1, at]
        m2 = m2 + 0.3 * still_ref[2, at]
        m3 = m3 + 0.3 * still_ref[3, at]
        for c in range(3):
            out_ref[c, at] = (
                coef_ref[c, 0] * m0 + coef_ref[c, 1] * m1 + coef_ref[c, 2] * m2 + coef_ref[c, 3] * m3
            )
        out_ref[3, at] = through


def over(pieces, order):
    total = 0.0
    for a, piece in enumerate(pieces):
        ahead = jnp.ones_like(piece[3])
        for b, other in enumerate(pieces):
            if a != b:
                ahead = ahead * jnp.where(order[b] < order[a], other[3], 1.0)
        total = total + piece[:3] * ahead[None]
    return total


def body(density, color_coef):
    cells, planes, lanes = density.shape
    light_count = lax.axis_size("light")
    view_count = lax.axis_size("view")
    light_scale = -2.0 / (lanes * light_count) * LOG2E
    view_scale = -2.0 / (cells * view_count) * LOG2E
    own_rows = planes // view_count
    chunk = 16
    rows = 32
    whole = pl.BlockSpec(memory_space=VMEM)

    totals, brick = pl.pallas_call(
        functools.partial(totals_kernel, chunk),
        out_shape=[
            jax.ShapeDtypeStruct((planes, cells), jnp.float32),
            jax.ShapeDtypeStruct(density.shape, density.dtype),
        ],
        in_specs=[pl.BlockSpec(memory_space=pl.ANY)],
        out_specs=[whole, whole],
        scratch_shapes=[pltpu.SemaphoreType.DMA((cells // chunk,))],
        compiler_params=pltpu.CompilerParams(vmem_limit_bytes=8 * 2**20),
    )(density)

    place = lax.axis_index("light")
    upstream = jnp.zeros_like(totals)
    arrived = [(mask, swapped(totals, "light", mask)) for mask in range(1, light_count)]

    shade, still = pl.pallas_call(
        functools.partial(local_kernel, rows, light_scale, view_scale),
        out_shape=[
            jax.ShapeDtypeStruct(density.shape, jnp.float32),
            jax.ShapeDtypeStruct((4, planes, lanes), jnp.float32),
        ],
        in_specs=[whole],
        out_specs=[whole, whole],
        compiler_params=pltpu.CompilerParams(vmem_limit_bytes=16 * 2**20),
        cost_estimate=pl.CostEstimate(
            flops=20 * cells * planes * lanes, bytes_accessed=2**23, transcendentals=2 * cells * planes * lanes
        ),
    )(brick)

    for mask, sums in arrived:
        upstream = upstream + jnp.where(place ^ mask < place, sums, 0.0)

    partial = pl.pallas_call(
        functools.partial(lit_kernel, rows, light_scale),
        out_shape=jax.ShapeDtypeStruct((4, planes, lanes), jnp.float32),
        in_specs=[pl.BlockSpec(memory_space=pltpu.SMEM), whole, whole, whole, whole],
        out_specs=whole,
        compiler_params=pltpu.CompilerParams(vmem_limit_bytes=16 * 2**20),
    )(color_coef, brick, shade, still, upstream)

    mine = lax.axis_index("view")
    split = partial.reshape(4, view_count // 2, 2, own_rows, lanes)
    core, chip = mine % 2, mine // 2
    keep = lax.dynamic_index_in_dim(split, core, 2, False)
    give = lax.dynamic_index_in_dim(split, 1 - core, 2, False)
    took = swapped(give, "view", 1)
    near = jnp.where(core == 0, keep, took)
    far = jnp.where(core == 0, took, keep)
    color = near[:3] + near[3][None] * far[:3]
    both = jnp.concatenate([color, (near[3] * far[3])[None]], axis=0)
    pieces = [lax.dynamic_index_in_dim(both, chip, 1, False)]
    order = [chip]
    for mask in range(1, view_count // 2):
        pieces.append(swapped(lax.dynamic_index_in_dim(both, chip ^ mask, 1, False), "view", 2 * mask))
        order.append(chip ^ mask)
    return over(pieces, order)


def solution(mesh):
    placed = (P("view", None, "light"), P())
    return jax.shard_map(
        body, mesh=mesh, in_specs=placed, out_specs=P(None, "view", "light"), check_vma=False
    )
```

```python
import functools
import math

import jax
import jax.numpy as jnp
import ml_dtypes
from jax import lax
from jax.experimental import pallas as pl
from jax.experimental.pallas import tpu as pltpu
from jax.sharding import PartitionSpec as P

VMEM = pltpu.VMEM
LOG2E = math.log2(math.e)
HEIGHT = 16


def swapped(x, axis, mask):
    devices = lax.axis_size(axis)
    return lax.ppermute(x, axis, [(i, i ^ mask) for i in range(devices)])


def in_parts(scale):
    high = float(ml_dtypes.bfloat16(scale))
    return high, float(ml_dtypes.bfloat16(scale - high))


def stacked(pattern, parts):
    return jnp.concatenate(
        [jnp.where(pattern, part, 0.0).astype(jnp.bfloat16) for part in parts], axis=0
    )


def totals_kernel(chunk, density_ref, totals_ref, brick_ref, sem):
    cells, planes, lanes = brick_ref.shape
    half = cells // 2
    copies = []
    for k in range(half // chunk):
        for first in (k * chunk, half + k * chunk):
            at = pl.ds(first, chunk)
            copies.append(
                pltpu.make_async_copy(density_ref.at[at], brick_ref.at[at], sem.at[len(copies)])
            )
            copies[-1].start()
    row = lax.broadcasted_iota(jnp.int32, (16, 2 * lanes), 0)
    column = lax.broadcasted_iota(jnp.int32, (16, 2 * lanes), 1)
    pick = jnp.where(row == column // lanes, 1.0, 0.0).astype(jnp.bfloat16)

    def pair(v):
        return [brick_ref[v], brick_ref[half + v]]

    for k in range(half // chunk):
        copies[2 * k].wait()
        copies[2 * k + 1].wait()
        for v in range(k * chunk, (k + 1) * chunk, 4):
            left = jnp.concatenate(pair(v) + pair(v + 1), axis=0)
            right = jnp.concatenate(pair(v + 2) + pair(v + 3), axis=0)
            sums = lax.dot_general(
                pick,
                jnp.concatenate([left, right], axis=1),
                (((1,), (1,)), ((), ())),
                preferred_element_type=jnp.float32,
            )
            for j in range(4):
                at = pl.ds(j % 2 * 2 * planes, 2 * planes)
                totals_ref[v + j : v + j + 1] = sums[j // 2 : j // 2 + 1, at.start : at.start + at.size]


def local_kernel(rows, step_cells, light_parts, view_parts, brick_ref, *refs):
    shade_ref, value_ref, still_ref, even, odd = refs
    cells, planes, lanes = brick_ref.shape
    chunks = cells // step_cells
    before = lax.broadcasted_iota(jnp.int32, (lanes, lanes), 0)
    after = lax.broadcasted_iota(jnp.int32, (lanes, lanes), 1)
    depths = jnp.concatenate(
        [stacked(before < after, light_parts), stacked(before == after, view_parts)], axis=1
    )

    def fill(chunk, at, buffer):
        packed = brick_ref[pl.ds(chunk * step_cells, step_cells), at]
        flat = packed.reshape(step_cells * rows, lanes)
        depth = jnp.dot(
            jnp.concatenate([flat, flat], axis=1), depths, preferred_element_type=jnp.float32
        )
        buffer[0] = jnp.exp2(depth[:, :lanes])
        buffer[1] = jnp.exp2(depth[:, lanes:])
        buffer[2] = depth[:, lanes:]

    def use(chunk, at, buffer, state):
        through, m1, m2, m3 = state
        for j in range(step_cells):
            cell = chunk * step_cells + j
            here = pl.ds(j * rows, rows)
            value = buffer[2, here]
            passed = through * buffer[1, here]
            weight = through - passed
            through = passed
            value_ref[cell, at] = value
            shade_ref[cell, at] = weight * buffer[0, here]
            weight = weight * value
            m1 = m1 + weight
            weight = weight * value
            m2 = m2 + weight
            weight = weight * value
            m3 = m3 + weight
        return through, m1, m2, m3

    blocks = [pl.ds(z, rows) for z in range(0, planes, rows)]
    fill(0, blocks[0], even)
    for k, at in enumerate(blocks):
        zero = jnp.zeros((rows, lanes), jnp.float32)
        state = (jnp.ones((rows, lanes), jnp.float32), zero, zero, zero)
        for chunk in range(0, chunks, 2):
            fill(chunk + 1, at, odd)
            state = use(chunk, at, even, state)
            if chunk + 2 < chunks:
                fill(chunk + 2, at, even)
            elif k + 1 < len(blocks):
                fill(0, blocks[k + 1], even)
            state = use(chunk + 1, at, odd, state)
        for i in range(4):
            still_ref[i, at] = state[i]


def lit_kernel(
    step_cells,
    light_scale,
    unit,
    coef_ref,
    light_ref,
    still_ref,
    shade_ref,
    value_ref,
    out_ref,
    reach_ref,
    even,
    odd,
):
    cells, planes, lanes = shade_ref.shape
    blocks = planes // HEIGHT
    chunks = cells // step_cells
    reach = jnp.exp2(light_ref[...] * light_scale).T
    half = reach.shape[0] // 2
    reach_ref[...] = jnp.concatenate([reach[:half], reach[half:]], axis=1)
    pair = lax.broadcasted_iota(jnp.int32, (HEIGHT, cells), 1) // 2
    row = lax.broadcasted_iota(jnp.int32, (2 * cells, 2 * lanes), 0)
    column = lax.broadcasted_iota(jnp.int32, (2 * cells, 2 * lanes), 1)
    turns = jnp.where((row % 2 == 0) == (column < lanes), 1.0, 0.0).astype(jnp.bfloat16)

    def parts(k):
        reach = reach_ref[pl.ds(k * HEIGHT, HEIGHT)]
        high = reach.astype(jnp.bfloat16)
        return high, (reach - high.astype(jnp.float32)).astype(jnp.bfloat16)

    def fill(chunk, both, buffer):
        first = chunk * step_cells // 2
        picked = [
            jnp.concatenate([jnp.where(pair == first + p, part, 0) for part in both], axis=1)
            for p in range(step_cells // 2)
        ]
        spread = jnp.dot(
            jnp.concatenate(picked, axis=0), turns, preferred_element_type=jnp.float32
        )
        buffer[0] = spread[:, :lanes]
        buffer[1] = spread[:, lanes:]

    def use(chunk, k, buffer, state):
        m0, m1, m2, m3 = state
        at = pl.ds(k * HEIGHT, HEIGHT)
        for j in range(step_cells):
            cell = chunk * step_cells + j
            value = value_ref[cell, at]
            weight = shade_ref[cell, at] * buffer[j % 2, pl.ds(j // 2 * HEIGHT, HEIGHT)]
            m0 = m0 + weight
            weight = weight * value
            m1 = m1 + weight
            weight = weight * value
            m2 = m2 + weight
            weight = weight * value
            m3 = m3 + weight
        return m0, m1, m2, m3

    both = parts(0)
    fill(0, both, even)
    for k in range(blocks):
        state = (jnp.zeros((HEIGHT, lanes), jnp.float32),) * 4
        for chunk in range(0, chunks, 2):
            fill(chunk + 1, both, odd)
            state = use(chunk, k, even, state)
            if chunk + 2 < chunks:
                fill(chunk + 2, both, even)
            elif k + 1 < blocks:
                both = parts(k + 1)
                fill(0, both, even)
            state = use(chunk + 1, k, odd, state)
        at = pl.ds(k * HEIGHT, HEIGHT)
        through = still_ref[0, at]
        m0 = state[0] + 0.3 * (1.0 - through)
        m1, m2, m3 = (state[i] + 0.3 * still_ref[i, at] for i in (1, 2, 3))
        for c in range(3):
            out_ref[k, c] = (
                coef_ref[c, 0] * m0
                + coef_ref[c, 1] * unit * m1
                + coef_ref[c, 2] * unit**2 * m2
                + coef_ref[c, 3] * unit**3 * m3
            )
        out_ref[k, 3] = through


def over(pieces, order):
    total = 0.0
    for a, piece in enumerate(pieces):
        ahead = jnp.ones_like(piece[3])
        for b, other in enumerate(pieces):
            if a != b:
                ahead = ahead * jnp.where(order[b] < order[a], other[3], 1.0)
        total = total + piece[:3] * ahead[None]
    return total


def body(density, color_coef):
    cells, planes, lanes = density.shape
    light_count = lax.axis_size("light")
    view_count = lax.axis_size("view")
    light_scale = -2.0 / (lanes * light_count) * LOG2E
    view_parts = in_parts(-2.0 / (cells * view_count) * LOG2E)
    own_rows = planes // view_count
    chunk = 32
    step_cells = 16
    rows = 32
    lit_cells = 16
    whole = pl.BlockSpec(memory_space=VMEM)
    scalars = pl.BlockSpec(memory_space=pltpu.SMEM)

    totals, brick = pl.pallas_call(
        functools.partial(totals_kernel, chunk),
        name="totals_kernel",
        out_shape=[
            jax.ShapeDtypeStruct((cells // 2, 2 * planes), jnp.float32),
            jax.ShapeDtypeStruct(density.shape, density.dtype),
        ],
        in_specs=[pl.BlockSpec(memory_space=pltpu.HBM)],
        out_specs=[whole, whole],
        scratch_shapes=[pltpu.SemaphoreType.DMA((cells // chunk,))],
        compiler_params=pltpu.CompilerParams(vmem_limit_bytes=50 * 2**20 + 2**19),
    )(density)

    place = lax.axis_index("light")
    arrived = [(mask, swapped(totals, "light", mask)) for mask in range(1, light_count)]

    mine = lax.axis_index("view")
    core, chip = mine % 2, mine // 2
    chips = view_count // 2
    others = list(range(1, chips))
    table = jax.ShapeDtypeStruct(density.shape, jnp.float32)
    shade, value, still = pl.pallas_call(
        functools.partial(local_kernel, rows, step_cells, in_parts(light_scale), view_parts),
        name="local_kernel",
        out_shape=[table, table, jax.ShapeDtypeStruct((4, planes, lanes), jnp.float32)],
        in_specs=[whole],
        out_specs=[whole] * 3,
        scratch_shapes=[VMEM((3, step_cells * rows, lanes), jnp.float32)] * 2,
        compiler_params=pltpu.CompilerParams(vmem_limit_bytes=8 * 2**20),
        cost_estimate=pl.CostEstimate(
            flops=20 * density.size, bytes_accessed=2**23, transcendentals=2 * density.size
        ),
    )(brick)

    upstream = jnp.zeros_like(totals)
    for mask, other in arrived:
        upstream = upstream + jnp.where(place ^ mask < place, other, 0.0)

    away = pl.pallas_call(
        functools.partial(lit_kernel, lit_cells, light_scale, 1.0 / sum(view_parts)),
        name="lit_kernel",
        out_shape=jax.ShapeDtypeStruct((planes // HEIGHT, 4, HEIGHT, lanes), jnp.float32),
        in_specs=[scalars] + [whole] * 4,
        out_specs=whole,
        scratch_shapes=[VMEM((planes, cells), jnp.float32)]
        + [VMEM((2, lit_cells // 2 * HEIGHT, lanes), jnp.float32)] * 2,
        compiler_params=pltpu.CompilerParams(vmem_limit_bytes=8 * 2**20),
    )(color_coef, upstream, still, shade, value)

    if 2 * own_rows != HEIGHT:
        away = jnp.swapaxes(away, 0, 1).reshape(4, chips, 2 * own_rows, lanes)
        away = jnp.swapaxes(away, 0, 1)
    sent = [lax.dynamic_index_in_dim(away, chip ^ mask, 0, False) for mask in others]
    own = lax.dynamic_index_in_dim(away, chip, 0, False)
    pieces = [own] + [swapped(x, "view", 2 * mask) for x, mask in zip(sent, others)]
    order = [chip] + [chip ^ mask for mask in others]
    pieces = jnp.stack(pieces).reshape(chips, 4, 2, own_rows, lanes)
    keep = lax.dynamic_index_in_dim(pieces, core, 2, False)
    took = swapped(lax.dynamic_index_in_dim(pieces, 1 - core, 2, False), "view", 1)
    near = jnp.where(core == 0, keep, took)
    far = jnp.where(core == 0, took, keep)
    color = near[:, :3] + near[:, 3:] * far[:, :3]
    both = jnp.concatenate([color, near[:, 3:] * far[:, 3:]], axis=1)
    return over([both[k] for k in range(chips)], order)


def solution(mesh):
    placed = (P("view", None, "light"), P())
    return jax.shard_map(
        body, mesh=mesh, in_specs=placed, out_specs=P(None, "view", "light"), check_vma=False
    )
```

```python
import functools
import math

import jax
import jax.numpy as jnp
import ml_dtypes
from jax import lax
from jax.experimental import pallas as pl
from jax.experimental.pallas import tpu as pltpu
from jax.sharding import PartitionSpec as P

VMEM = pltpu.VMEM
LOG2E = math.log2(math.e)
HEIGHT = 16


def swapped(x, axis, mask):
    devices = lax.axis_size(axis)
    return lax.ppermute(x, axis, [(i, i ^ mask) for i in range(devices)])


def in_parts(scale):
    high = float(ml_dtypes.bfloat16(scale))
    return high, float(ml_dtypes.bfloat16(scale - high))


def stacked(pattern, parts):
    return jnp.concatenate(
        [jnp.where(pattern, part, 0.0).astype(jnp.bfloat16) for part in parts], axis=0
    )


def chunk_copies(chunk, density_ref, brick_ref, sem):
    half = brick_ref.shape[0] // 2
    copies = []
    for k in range(half // chunk):
        for first in (k * chunk, half + k * chunk):
            at = pl.ds(first, chunk)
            copies.append(
                pltpu.make_async_copy(density_ref.at[at], brick_ref.at[at], sem.at[len(copies)])
            )
    return copies


def totals_kernel(chunk, last, place_ref, density_ref, totals_ref, brick_ref, sem):
    cells, planes, lanes = brick_ref.shape
    half = cells // 2

    @pl.when(place_ref[0] == last)
    def _():
        totals_ref[...] = jnp.zeros_like(totals_ref)

    @pl.when(place_ref[0] != last)
    def _():
        copies = chunk_copies(chunk, density_ref, brick_ref, sem)
        for copy in copies:
            copy.start()
        row = lax.broadcasted_iota(jnp.int32, (16, 2 * lanes), 0)
        column = lax.broadcasted_iota(jnp.int32, (16, 2 * lanes), 1)
        pick = jnp.where(row == column // lanes, 1.0, 0.0).astype(jnp.bfloat16)

        def pair(v):
            return [brick_ref[v], brick_ref[half + v]]

        for k in range(half // chunk):
            copies[2 * k].wait()
            copies[2 * k + 1].wait()
            for v in range(k * chunk, (k + 1) * chunk, 4):
                left = jnp.concatenate(pair(v) + pair(v + 1), axis=0)
                right = jnp.concatenate(pair(v + 2) + pair(v + 3), axis=0)
                sums = lax.dot_general(
                    pick,
                    jnp.concatenate([left, right], axis=1),
                    (((1,), (1,)), ((), ())),
                    preferred_element_type=jnp.float32,
                )
                for j in range(4):
                    first = j % 2 * 2 * planes
                    totals_ref[v + j : v + j + 1] = sums[
                        j // 2 : j // 2 + 1, first : first + 2 * planes
                    ]


def brick_kernel(chunk, last, place_ref, density_ref, brick_in_ref, brick_ref, sem):
    @pl.when(place_ref[0] == last)
    def _():
        copies = chunk_copies(chunk, density_ref, brick_ref, sem)
        for copy in copies:
            copy.start()
        for copy in copies:
            copy.wait()


def local_kernel(
    rows,
    step_cells,
    light_parts,
    view_parts,
    place_ref,
    brick_ref,
    shade_ref,
    value_ref,
    still_ref,
    even,
    odd,
):
    cells, planes, lanes = brick_ref.shape
    chunks = cells // step_cells
    before = lax.broadcasted_iota(jnp.int32, (lanes, lanes), 0)
    after = lax.broadcasted_iota(jnp.int32, (lanes, lanes), 1)
    depths = jnp.concatenate(
        [stacked(before < after, light_parts), stacked(before == after, view_parts)], axis=1
    )

    def fill(chunk, at, buffer):
        packed = brick_ref[pl.ds(chunk * step_cells, step_cells), at]
        flat = packed.reshape(step_cells * rows, lanes)
        depth = jnp.dot(
            jnp.concatenate([flat, flat], axis=1), depths, preferred_element_type=jnp.float32
        )
        buffer[0] = jnp.exp2(depth[:, :lanes])
        buffer[1] = jnp.exp2(depth[:, lanes:])
        buffer[2] = depth[:, lanes:]

    def use(chunk, at, buffer, state, first):
        through, *moments = state
        for j in range(step_cells):
            cell = chunk * step_cells + j
            here = pl.ds(j * rows, rows)
            value = buffer[2, here]
            passed = through * buffer[1, here]
            weight = through - passed
            through = passed
            if first:
                weight = weight * (0.3 + buffer[0, here])
                moments[0] = moments[0] + weight
            else:
                value_ref[cell, at] = value
                shade_ref[cell, at] = weight * buffer[0, here]
            for i in (1, 2, 3):
                weight = weight * value
                moments[i] = moments[i] + weight
        return through, *moments

    def run(first):
        blocks = [pl.ds(z, rows) for z in range(0, planes, rows)]
        fill(0, blocks[0], even)
        for k, at in enumerate(blocks):
            zero = jnp.zeros((rows, lanes), jnp.float32)
            state = (jnp.ones((rows, lanes), jnp.float32), zero, zero, zero, zero)
            for chunk in range(0, chunks, 2):
                fill(chunk + 1, at, odd)
                state = use(chunk, at, even, state, first)
                if chunk + 2 < chunks:
                    fill(chunk + 2, at, even)
                elif k + 1 < len(blocks):
                    fill(0, blocks[k + 1], even)
                state = use(chunk + 1, at, odd, state, first)
            for i in range(5):
                still_ref[i, at] = state[i]

    @pl.when(place_ref[0] == 0)
    def _():
        run(True)

    @pl.when(place_ref[0] != 0)
    def _():
        run(False)


def lit_kernel(
    step_cells,
    light_scale,
    unit,
    place_ref,
    coef_ref,
    light_ref,
    still_ref,
    shade_ref,
    value_ref,
    out_ref,
    reach_ref,
    even,
    odd,
):
    cells, planes, lanes = shade_ref.shape
    blocks = planes // HEIGHT
    chunks = cells // step_cells
    def finish(k, moments):
        through = still_ref[0, pl.ds(k * HEIGHT, HEIGHT)]
        for c in range(3):
            out_ref[k, c] = (
                coef_ref[c, 0] * moments[0]
                + coef_ref[c, 1] * unit * moments[1]
                + coef_ref[c, 2] * unit**2 * moments[2]
                + coef_ref[c, 3] * unit**3 * moments[3]
            )
        out_ref[k, 3] = through

    pair = lax.broadcasted_iota(jnp.int32, (HEIGHT, cells), 1) // 2
    row = lax.broadcasted_iota(jnp.int32, (2 * cells, 2 * lanes), 0)
    column = lax.broadcasted_iota(jnp.int32, (2 * cells, 2 * lanes), 1)
    turns = jnp.where((row % 2 == 0) == (column < lanes), 1.0, 0.0).astype(jnp.bfloat16)

    def parts(k):
        reach = reach_ref[pl.ds(k * HEIGHT, HEIGHT)]
        high = reach.astype(jnp.bfloat16)
        return high, (reach - high.astype(jnp.float32)).astype(jnp.bfloat16)

    def fill(chunk, both, buffer):
        first = chunk * step_cells // 2
        picked = [
            jnp.concatenate([jnp.where(pair == first + p, part, 0) for part in both], axis=1)
            for p in range(step_cells // 2)
        ]
        spread = jnp.dot(
            jnp.concatenate(picked, axis=0), turns, preferred_element_type=jnp.float32
        )
        buffer[0] = spread[:, :lanes]
        buffer[1] = spread[:, lanes:]

    def use(chunk, k, buffer, state):
        m0, m1, m2, m3 = state
        at = pl.ds(k * HEIGHT, HEIGHT)
        for j in range(step_cells):
            cell = chunk * step_cells + j
            value = value_ref[cell, at]
            weight = shade_ref[cell, at] * buffer[j % 2, pl.ds(j // 2 * HEIGHT, HEIGHT)]
            m0 = m0 + weight
            weight = weight * value
            m1 = m1 + weight
            weight = weight * value
            m2 = m2 + weight
            weight = weight * value
            m3 = m3 + weight
        return m0, m1, m2, m3

    @pl.when(place_ref[0] == 0)
    def _():
        for k in range(blocks):
            finish(k, [still_ref[1 + i, pl.ds(k * HEIGHT, HEIGHT)] for i in range(4)])

    @pl.when(place_ref[0] != 0)
    def _():
        reach = jnp.exp2(light_ref[...] * light_scale).T
        half = reach.shape[0] // 2
        reach_ref[...] = jnp.concatenate([reach[:half], reach[half:]], axis=1)
        both = parts(0)
        fill(0, both, even)
        for k in range(blocks):
            state = (jnp.zeros((HEIGHT, lanes), jnp.float32),) * 4
            for chunk in range(0, chunks, 2):
                fill(chunk + 1, both, odd)
                state = use(chunk, k, even, state)
                if chunk + 2 < chunks:
                    fill(chunk + 2, both, even)
                elif k + 1 < blocks:
                    both = parts(k + 1)
                    fill(0, both, even)
                state = use(chunk + 1, k, odd, state)
            at = pl.ds(k * HEIGHT, HEIGHT)
            m0 = state[0] + 0.3 * (1.0 - still_ref[0, at])
            finish(k, [m0] + [state[i] + 0.3 * still_ref[1 + i, at] for i in (1, 2, 3)])


def over(pieces, order):
    total = 0.0
    for a, piece in enumerate(pieces):
        ahead = jnp.ones_like(piece[3])
        for b, other in enumerate(pieces):
            if a != b:
                ahead = ahead * jnp.where(order[b] < order[a], other[3], 1.0)
        total = total + piece[:3] * ahead[None]
    return total


def body(density, color_coef):
    cells, planes, lanes = density.shape
    light_count = lax.axis_size("light")
    view_count = lax.axis_size("view")
    light_scale = -2.0 / (lanes * light_count) * LOG2E
    view_parts = in_parts(-2.0 / (cells * view_count) * LOG2E)
    own_rows = planes // view_count
    chunk = 32
    step_cells = 16
    rows = 32
    lit_cells = 16
    whole = pl.BlockSpec(memory_space=VMEM)
    scalars = pl.BlockSpec(memory_space=pltpu.SMEM)

    place = lax.axis_index("light")
    where = place.astype(jnp.int32)[None]
    brick_shape = jax.ShapeDtypeStruct(density.shape, density.dtype)
    sem = pltpu.SemaphoreType.DMA((cells // chunk,))
    wide = pltpu.CompilerParams(vmem_limit_bytes=50 * 2**20 + 2**19)
    totals, brick = pl.pallas_call(
        functools.partial(totals_kernel, chunk, light_count - 1),
        name="totals_kernel",
        out_shape=[jax.ShapeDtypeStruct((cells // 2, 2 * planes), jnp.float32), brick_shape],
        in_specs=[scalars, pl.BlockSpec(memory_space=pltpu.HBM)],
        out_specs=[whole, whole],
        scratch_shapes=[sem],
        compiler_params=wide,
    )(where, density)

    arrived = [(mask, swapped(totals, "light", mask)) for mask in range(light_count - 1, 0, -1)]

    brick = pl.pallas_call(
        functools.partial(brick_kernel, chunk, light_count - 1),
        name="brick_kernel",
        out_shape=brick_shape,
        in_specs=[scalars, pl.BlockSpec(memory_space=pltpu.HBM), whole],
        out_specs=whole,
        input_output_aliases={2: 0},
        scratch_shapes=[sem],
        compiler_params=wide,
    )(where, density, brick)

    mine = lax.axis_index("view")
    core, chip = mine % 2, mine // 2
    chips = view_count // 2
    others = list(range(chips - 1, 0, -1))
    table = jax.ShapeDtypeStruct(density.shape, jnp.float32)
    shade, value, still = pl.pallas_call(
        functools.partial(local_kernel, rows, step_cells, in_parts(light_scale), view_parts),
        name="local_kernel",
        out_shape=[table, table, jax.ShapeDtypeStruct((5, planes, lanes), jnp.float32)],
        in_specs=[scalars, whole],
        out_specs=[whole] * 3,
        scratch_shapes=[VMEM((3, step_cells * rows, lanes), jnp.float32)] * 2,
        compiler_params=pltpu.CompilerParams(vmem_limit_bytes=8 * 2**20),
        cost_estimate=pl.CostEstimate(
            flops=20 * density.size, bytes_accessed=2**23, transcendentals=2 * density.size
        ),
    )(where, brick)

    upstream = jnp.zeros_like(totals)
    for mask, other in arrived:
        upstream = upstream + jnp.where(place ^ mask < place, other, 0.0)

    away = pl.pallas_call(
        functools.partial(lit_kernel, lit_cells, light_scale, 1.0 / sum(view_parts)),
        name="lit_kernel",
        out_shape=jax.ShapeDtypeStruct((planes // HEIGHT, 4, HEIGHT, lanes), jnp.float32),
        in_specs=[scalars] * 2 + [whole] * 4,
        out_specs=whole,
        scratch_shapes=[VMEM((planes, cells), jnp.float32)]
        + [VMEM((2, lit_cells // 2 * HEIGHT, lanes), jnp.float32)] * 2,
        compiler_params=pltpu.CompilerParams(vmem_limit_bytes=8 * 2**20),
    )(where, color_coef, upstream, still, shade, value)

    if 2 * own_rows != HEIGHT:
        away = jnp.swapaxes(away, 0, 1).reshape(4, chips, 2 * own_rows, lanes)
        away = jnp.swapaxes(away, 0, 1)
    sent = [lax.dynamic_index_in_dim(away, chip ^ mask, 0, False) for mask in others]
    own = lax.dynamic_index_in_dim(away, chip, 0, False)
    pieces = [own] + [swapped(x, "view", 2 * mask) for x, mask in zip(sent, others)]
    order = [chip] + [chip ^ mask for mask in others]
    pieces = jnp.stack(pieces).reshape(chips, 4, 2, own_rows, lanes)
    keep = lax.dynamic_index_in_dim(pieces, core, 2, False)
    took = swapped(lax.dynamic_index_in_dim(pieces, 1 - core, 2, False), "view", 1)
    near = jnp.where(core == 0, keep, took)
    far = jnp.where(core == 0, took, keep)
    color = near[:, :3] + near[:, 3:] * far[:, :3]
    both = jnp.concatenate([color, near[:, 3:] * far[:, 3:]], axis=1)
    return over([both[k] for k in range(chips)], order)


def solution(mesh):
    placed = (P("view", None, "light"), P())
    return jax.shard_map(
        body, mesh=mesh, in_specs=placed, out_specs=P(None, "view", "light"), check_vma=False
    )
```

```python
import functools
import math

import jax
import jax.numpy as jnp
import ml_dtypes
from jax import lax
from jax.experimental import pallas as pl
from jax.experimental.pallas import tpu as pltpu
from jax.sharding import PartitionSpec as P

VMEM = pltpu.VMEM
LOG2E = math.log2(math.e)
HEIGHT = 16


def swapped(x, axis, mask):
    devices = lax.axis_size(axis)
    return lax.ppermute(x, axis, [(i, i ^ mask) for i in range(devices)])


def in_parts(scale):
    high = float(ml_dtypes.bfloat16(scale))
    return high, float(ml_dtypes.bfloat16(scale - high))


def stacked(pattern, parts):
    return jnp.concatenate(
        [jnp.where(pattern, part, 0.0).astype(jnp.bfloat16) for part in parts], axis=0
    )


def chunk_copies(chunk, density_ref, brick_ref, sem):
    half = brick_ref.shape[0] // 2
    copies = []
    for k in range(half // chunk):
        for first in (k * chunk, half + k * chunk):
            at = pl.ds(first, chunk)
            copies.append(
                pltpu.make_async_copy(density_ref.at[at], brick_ref.at[at], sem.at[len(copies)])
            )
    return copies


def totals_kernel(chunk, last, place_ref, density_ref, totals_ref, brick_ref, sem):
    cells, planes, lanes = brick_ref.shape
    half = cells // 2

    @pl.when(place_ref[0] == last)
    def _():
        totals_ref[...] = jnp.zeros_like(totals_ref)

    @pl.when(place_ref[0] != last)
    def _():
        copies = chunk_copies(chunk, density_ref, brick_ref, sem)
        for copy in copies:
            copy.start()
        row = lax.broadcasted_iota(jnp.int32, (16, 2 * lanes), 0)
        column = lax.broadcasted_iota(jnp.int32, (16, 2 * lanes), 1)
        pick = jnp.where(row == column // lanes, 1.0, 0.0).astype(jnp.bfloat16)

        def pair(v):
            return [brick_ref[v], brick_ref[half + v]]

        for k in range(half // chunk):
            copies[2 * k].wait()
            copies[2 * k + 1].wait()
            for v in range(k * chunk, (k + 1) * chunk, 4):
                left = jnp.concatenate(pair(v) + pair(v + 1), axis=0)
                right = jnp.concatenate(pair(v + 2) + pair(v + 3), axis=0)
                sums = lax.dot_general(
                    pick,
                    jnp.concatenate([left, right], axis=1),
                    (((1,), (1,)), ((), ())),
                    preferred_element_type=jnp.float32,
                )
                for j in range(4):
                    first = j % 2 * 2 * planes
                    totals_ref[v + j : v + j + 1] = sums[
                        j // 2 : j // 2 + 1, first : first + 2 * planes
                    ]


def brick_kernel(chunk, last, place_ref, density_ref, brick_in_ref, brick_ref, sem):
    @pl.when(place_ref[0] == last)
    def _():
        copies = chunk_copies(chunk, density_ref, brick_ref, sem)
        for copy in copies:
            copy.start()
        for copy in copies:
            copy.wait()


def local_kernel(
    rows,
    step_cells,
    light_parts,
    view_parts,
    place_ref,
    brick_ref,
    shade_ref,
    value_ref,
    still_ref,
):
    cells, planes, lanes = brick_ref.shape
    chunks = cells // step_cells
    before = lax.broadcasted_iota(jnp.int32, (lanes, lanes), 0)
    after = lax.broadcasted_iota(jnp.int32, (lanes, lanes), 1)
    depths = jnp.concatenate(
        [stacked(before < after, light_parts), stacked(before == after, view_parts)], axis=1
    )

    def fill(chunk, at):
        packed = brick_ref[pl.ds(chunk * step_cells, step_cells), at]
        flat = packed.reshape(step_cells * rows, lanes)
        depth = jnp.dot(
            jnp.concatenate([flat, flat], axis=1), depths, preferred_element_type=jnp.float32
        )
        return jnp.exp2(depth[:, :lanes]), jnp.exp2(depth[:, lanes:]), depth[:, lanes:]

    def use(chunk, at, buffer, state, first):
        through, *moments = state
        for j in range(step_cells):
            cell = chunk * step_cells + j
            lit, pass_on, value = (x[j * rows : (j + 1) * rows] for x in buffer)
            passed = through * pass_on
            weight = through - passed
            through = passed
            if first:
                weight = weight * (0.3 + lit)
                moments[0] = moments[0] + weight
            else:
                value_ref[cell, at] = value
                shade_ref[cell, at] = weight * lit
            for i in (1, 2, 3):
                weight = weight * value
                moments[i] = moments[i] + weight
        return through, *moments

    def run(first):
        blocks = [pl.ds(z, rows) for z in range(0, planes, rows)]
        for k, at in enumerate(blocks):
            zero = jnp.zeros((rows, lanes), jnp.float32)
            state = (jnp.ones((rows, lanes), jnp.float32), zero, zero, zero, zero)
            for chunk in range(chunks):
                state = use(chunk, at, fill(chunk, at), state, first)
            for i in range(5):
                still_ref[i, at] = state[i]

    @pl.when(place_ref[0] == 0)
    def _():
        run(True)

    @pl.when(place_ref[0] != 0)
    def _():
        run(False)


def lit_kernel(
    step_cells,
    light_scale,
    unit,
    place_ref,
    coef_ref,
    light_ref,
    still_ref,
    shade_ref,
    value_ref,
    out_ref,
    reach_ref,
):
    cells, planes, lanes = shade_ref.shape
    blocks = planes // HEIGHT
    chunks = cells // step_cells
    def block_rows(k):
        return pl.ds(k * HEIGHT if isinstance(k, int) else pl.multiple_of(k * HEIGHT, HEIGHT), HEIGHT)

    def finish(k, moments):
        through = still_ref[0, block_rows(k)]
        for c in range(3):
            out_ref[k, c] = sum(
                coef_ref[c : c + 1, i : i + 1] * unit**i * moments[i] for i in range(4)
            )
        out_ref[k, 3] = through

    def parts(k):
        reach = reach_ref[block_rows(k)]
        high = reach.astype(jnp.bfloat16)
        return high, (reach - high.astype(jnp.float32)).astype(jnp.bfloat16)

    def fill(chunk, both, pair, turns):
        first = chunk * step_cells // 2
        picked = [
            jnp.concatenate([jnp.where(pair == first + p, part, 0) for part in both], axis=1)
            for p in range(step_cells // 2)
        ]
        spread = jnp.dot(
            jnp.concatenate(picked, axis=0), turns, preferred_element_type=jnp.float32
        )
        return spread[:, :lanes], spread[:, lanes:]

    def use(chunk, k, spread, state):
        m0, m1, m2, m3 = state
        at = block_rows(k)
        for j in range(step_cells):
            cell = chunk * step_cells + j
            value = value_ref[cell, at]
            here = slice(j // 2 * HEIGHT, (j // 2 + 1) * HEIGHT)
            weight = shade_ref[cell, at] * spread[j % 2][here]
            m0 = m0 + weight
            weight = weight * value
            m1 = m1 + weight
            weight = weight * value
            m2 = m2 + weight
            weight = weight * value
            m3 = m3 + weight
        return m0, m1, m2, m3

    @pl.when(place_ref[0] == 0)
    def _():
        for k in range(blocks):
            finish(k, [still_ref[1 + i, block_rows(k)] for i in range(4)])

    @pl.when(place_ref[0] != 0)
    def _():
        pair = lax.broadcasted_iota(jnp.int32, (HEIGHT, cells), 1) // 2
        row = lax.broadcasted_iota(jnp.int32, (2 * cells, 2 * lanes), 0)
        column = lax.broadcasted_iota(jnp.int32, (2 * cells, 2 * lanes), 1)
        turns = jnp.where((row % 2 == 0) == (column < lanes), 1.0, 0.0).astype(jnp.bfloat16)
        reach = jnp.exp2(light_ref[...] * light_scale).T
        half = reach.shape[0] // 2
        reach_ref[...] = jnp.concatenate([reach[:half], reach[half:]], axis=1)
        for k in range(blocks):
            both = parts(k)
            state = (jnp.zeros((HEIGHT, lanes), jnp.float32),) * 4
            for chunk in range(chunks):
                state = use(chunk, k, fill(chunk, both, pair, turns), state)
            at = block_rows(k)
            m0 = state[0] + 0.3 * (1.0 - still_ref[0, at])
            finish(k, [m0] + [state[i] + 0.3 * still_ref[1 + i, at] for i in (1, 2, 3)])


def over(pieces, order):
    total = 0.0
    for a, piece in enumerate(pieces):
        ahead = jnp.ones_like(piece[3])
        for b, other in enumerate(pieces):
            if a != b:
                ahead = ahead * jnp.where(order[b] < order[a], other[3], 1.0)
        total = total + piece[:3] * ahead[None]
    return total


def body(density, color_coef):
    cells, planes, lanes = density.shape
    light_count = lax.axis_size("light")
    view_count = lax.axis_size("view")
    light_scale = -2.0 / (lanes * light_count) * LOG2E
    view_parts = in_parts(-2.0 / (cells * view_count) * LOG2E)
    own_rows = planes // view_count
    chunk = 32
    step_cells = 32
    rows = 16
    lit_cells = 32
    whole = pl.BlockSpec(memory_space=VMEM)
    scalars = pl.BlockSpec(memory_space=pltpu.SMEM)

    place = lax.axis_index("light")
    where = place.astype(jnp.int32)[None]
    brick_shape = jax.ShapeDtypeStruct(density.shape, density.dtype)
    sem = pltpu.SemaphoreType.DMA((cells // chunk,))
    wide = pltpu.CompilerParams(vmem_limit_bytes=50 * 2**20 + 2**19)
    totals, brick = pl.pallas_call(
        functools.partial(totals_kernel, chunk, light_count - 1),
        name="totals_kernel",
        out_shape=[jax.ShapeDtypeStruct((cells // 2, 2 * planes), jnp.float32), brick_shape],
        in_specs=[scalars, pl.BlockSpec(memory_space=pltpu.HBM)],
        out_specs=[whole, whole],
        scratch_shapes=[sem],
        compiler_params=wide,
    )(where, density)

    arrived = [(mask, swapped(totals, "light", mask)) for mask in range(light_count - 1, 0, -1)]

    brick = pl.pallas_call(
        functools.partial(brick_kernel, chunk, light_count - 1),
        name="brick_kernel",
        out_shape=brick_shape,
        in_specs=[scalars, pl.BlockSpec(memory_space=pltpu.HBM), whole],
        out_specs=whole,
        input_output_aliases={2: 0},
        scratch_shapes=[sem],
        compiler_params=wide,
    )(where, density, brick)

    mine = lax.axis_index("view")
    core, chip = mine % 2, mine // 2
    chips = view_count // 2
    others = list(range(chips - 1, 0, -1))
    table = jax.ShapeDtypeStruct(density.shape, jnp.float32)
    shade, value, still = pl.pallas_call(
        functools.partial(local_kernel, rows, step_cells, in_parts(light_scale), view_parts),
        name="local_kernel",
        out_shape=[table, table, jax.ShapeDtypeStruct((5, planes, lanes), jnp.float32)],
        in_specs=[scalars, whole],
        out_specs=[whole] * 3,
        compiler_params=pltpu.CompilerParams(vmem_limit_bytes=8 * 2**20),
        cost_estimate=pl.CostEstimate(
            flops=20 * density.size, bytes_accessed=2**23, transcendentals=2 * density.size
        ),
    )(where, brick)

    upstream = jnp.zeros_like(totals)
    for mask, other in arrived:
        upstream = upstream + jnp.where(place ^ mask < place, other, 0.0)

    away = pl.pallas_call(
        functools.partial(lit_kernel, lit_cells, light_scale, 1.0 / sum(view_parts)),
        name="lit_kernel",
        out_shape=jax.ShapeDtypeStruct((planes // HEIGHT, 4, HEIGHT, lanes), jnp.float32),
        in_specs=[scalars] + [whole] * 5,
        out_specs=whole,
        scratch_shapes=[VMEM((planes, cells), jnp.float32)],
        compiler_params=pltpu.CompilerParams(vmem_limit_bytes=8 * 2**20),
    )(where, color_coef, upstream, still, shade, value)

    if 2 * own_rows != HEIGHT:
        away = jnp.swapaxes(away, 0, 1).reshape(4, chips, 2 * own_rows, lanes)
        away = jnp.swapaxes(away, 0, 1)
    sent = [lax.dynamic_index_in_dim(away, chip ^ mask, 0, False) for mask in others]
    own = lax.dynamic_index_in_dim(away, chip, 0, False)
    pieces = [own] + [swapped(x, "view", 2 * mask) for x, mask in zip(sent, others)]
    order = [chip] + [chip ^ mask for mask in others]
    pieces = jnp.stack(pieces).reshape(chips, 4, 2, own_rows, lanes)
    keep = lax.dynamic_index_in_dim(pieces, core, 2, False)
    took = swapped(lax.dynamic_index_in_dim(pieces, 1 - core, 2, False), "view", 1)
    near = jnp.where(core == 0, keep, took)
    far = jnp.where(core == 0, took, keep)
    color = near[:, :3] + near[:, 3:] * far[:, :3]
    both = jnp.concatenate([color, near[:, 3:] * far[:, 3:]], axis=1)
    return over([both[k] for k in range(chips)], order)


def solution(mesh):
    placed = (P("view", None, "light"), P())
    return jax.shard_map(
        body, mesh=mesh, in_specs=placed, out_specs=P(None, "view", "light"), check_vma=False
    )
```

```python
import functools
import math

import jax
import jax.numpy as jnp
import ml_dtypes
from jax import lax
from jax.experimental import pallas as pl
from jax.experimental.pallas import tpu as pltpu
from jax.sharding import PartitionSpec as P

VMEM = pltpu.VMEM
LOG2E = math.log2(math.e)
HEIGHT = 16


def swapped(x, axis, mask):
    devices = lax.axis_size(axis)
    return lax.ppermute(x, axis, [(i, i ^ mask) for i in range(devices)])


def in_parts(scale):
    high = float(ml_dtypes.bfloat16(scale))
    return high, float(ml_dtypes.bfloat16(scale - high))


def stacked(pattern, parts):
    return jnp.concatenate(
        [jnp.where(pattern, part, 0.0).astype(jnp.bfloat16) for part in parts], axis=0
    )


def chunk_copies(chunk, density_ref, brick_ref, sem):
    half = brick_ref.shape[0] // 2
    copies = []
    for k in range(half // chunk):
        for first in (k * chunk, half + k * chunk):
            at = pl.ds(first, chunk)
            copies.append(
                pltpu.make_async_copy(density_ref.at[at], brick_ref.at[at], sem.at[len(copies)])
            )
    return copies


def totals_kernel(chunk, last, place_ref, density_ref, totals_ref, brick_ref, sem):
    cells, planes, lanes = brick_ref.shape
    half = cells // 2

    @pl.when(place_ref[0] == last)
    def _():
        totals_ref[...] = jnp.zeros_like(totals_ref)

    @pl.when(place_ref[0] != last)
    def _():
        copies = chunk_copies(chunk, density_ref, brick_ref, sem)
        for copy in copies:
            copy.start()
        row = lax.broadcasted_iota(jnp.int32, (16, 2 * lanes), 0)
        column = lax.broadcasted_iota(jnp.int32, (16, 2 * lanes), 1)
        pick = jnp.where(row == column // lanes, 1.0, 0.0).astype(jnp.bfloat16)

        def pair(v):
            return [brick_ref[v], brick_ref[half + v]]

        for k in range(half // chunk):
            copies[2 * k].wait()
            copies[2 * k + 1].wait()
            for v in range(k * chunk, (k + 1) * chunk, 4):
                left = jnp.concatenate(pair(v) + pair(v + 1), axis=0)
                right = jnp.concatenate(pair(v + 2) + pair(v + 3), axis=0)
                sums = lax.dot_general(
                    pick,
                    jnp.concatenate([left, right], axis=1),
                    (((1,), (1,)), ((), ())),
                    preferred_element_type=jnp.float32,
                )
                for j in range(4):
                    first = j % 2 * 2 * planes
                    totals_ref[v + j : v + j + 1] = sums[
                        j // 2 : j // 2 + 1, first : first + 2 * planes
                    ]


def brick_kernel(chunk, last, place_ref, density_ref, brick_in_ref, brick_ref, sem):
    @pl.when(place_ref[0] == last)
    def _():
        copies = chunk_copies(chunk, density_ref, brick_ref, sem)
        for copy in copies:
            copy.start()
        for copy in copies:
            copy.wait()


def local_kernel(
    rows,
    step_cells,
    light_parts,
    view_parts,
    place_ref,
    brick_ref,
    shade_ref,
    value_ref,
    still_ref,
):
    cells, planes, lanes = brick_ref.shape
    chunks = cells // step_cells
    before = lax.broadcasted_iota(jnp.int32, (lanes, lanes), 0)
    after = lax.broadcasted_iota(jnp.int32, (lanes, lanes), 1)
    depths = jnp.concatenate(
        [stacked(before < after, light_parts), stacked(before == after, view_parts)], axis=1
    )

    def fill(chunk, at):
        packed = brick_ref[pl.ds(chunk * step_cells, step_cells), at]
        flat = packed.reshape(step_cells * rows, lanes)
        depth = jnp.dot(
            jnp.concatenate([flat, flat], axis=1), depths, preferred_element_type=jnp.float32
        )
        return jnp.exp2(depth[:, :lanes]), jnp.exp2(depth[:, lanes:]), depth[:, lanes:]

    def use(chunk, at, buffer, state, first):
        through, *moments = state
        for j in range(step_cells):
            cell = chunk * step_cells + j
            lit, pass_on, value = (x[j * rows : (j + 1) * rows] for x in buffer)
            passed = through * pass_on
            weight = through - passed
            through = passed
            if first:
                weight = weight * (0.3 + lit)
                moments[0] = moments[0] + weight
            else:
                value_ref[cell, at] = value
                shade_ref[cell, at] = weight * lit
            for i in (1, 2, 3):
                weight = weight * value
                moments[i] = moments[i] + weight
        return through, *moments

    def run(first):
        blocks = [pl.ds(z, rows) for z in range(0, planes, rows)]
        for k, at in enumerate(blocks):
            zero = jnp.zeros((rows, lanes), jnp.float32)
            state = (jnp.ones((rows, lanes), jnp.float32), zero, zero, zero, zero)
            for chunk in range(chunks):
                state = use(chunk, at, fill(chunk, at), state, first)
            for i in range(5):
                still_ref[i, at] = state[i]

    @pl.when(place_ref[0] == 0)
    def _():
        run(True)

    @pl.when(place_ref[0] != 0)
    def _():
        run(False)


def lit_kernel(
    step_cells,
    light_scale,
    unit,
    picks,
    own,
    place_ref,
    chip_ref,
    coef_ref,
    light_ref,
    still_ref,
    shade_ref,
    value_ref,
    *refs,
):
    outs, refs = refs[: len(picks)], refs[len(picks) :]
    passed, (reach_ref,) = refs[:-1], refs[-1:]
    cells, _, lanes = shade_ref.shape
    chunks = cells // step_cells

    def block_rows(pick):
        if own is None:
            return pl.ds(pick * HEIGHT, HEIGHT)
        return pl.ds(pl.multiple_of((chip_ref[0] ^ pick) * HEIGHT, HEIGHT), HEIGHT)

    def finish(out_ref, at, moments):
        for c in range(3):
            out_ref[c] = sum(
                coef_ref[c : c + 1, i : i + 1] * unit**i * moments[i] for i in range(4)
            )
        out_ref[3] = still_ref[0, at]

    def parts(at):
        reach = reach_ref[at]
        high = reach.astype(jnp.bfloat16)
        return high, (reach - high.astype(jnp.float32)).astype(jnp.bfloat16)

    def fill(chunk, both, pair, turns):
        first = chunk * step_cells // 2
        picked = [
            jnp.concatenate([jnp.where(pair == first + p, part, 0) for part in both], axis=1)
            for p in range(step_cells // 2)
        ]
        spread = jnp.dot(
            jnp.concatenate(picked, axis=0), turns, preferred_element_type=jnp.float32
        )
        return spread[:, :lanes], spread[:, lanes:]

    def use(chunk, at, spread, state):
        m0, m1, m2, m3 = state
        for j in range(step_cells):
            cell = chunk * step_cells + j
            value = value_ref[cell, at]
            here = slice(j // 2 * HEIGHT, (j // 2 + 1) * HEIGHT)
            weight = shade_ref[cell, at] * spread[j % 2][here]
            m0 = m0 + weight
            weight = weight * value
            m1 = m1 + weight
            weight = weight * value
            m2 = m2 + weight
            weight = weight * value
            m3 = m3 + weight
        return m0, m1, m2, m3

    @pl.when(place_ref[0] == 0)
    def _():
        for pick, out_ref in zip(picks, outs):
            at = block_rows(pick)
            finish(out_ref, at, [still_ref[1 + i, at] for i in range(4)])

    @pl.when(place_ref[0] != 0)
    def _():
        pair = lax.broadcasted_iota(jnp.int32, (HEIGHT, cells), 1) // 2
        row = lax.broadcasted_iota(jnp.int32, (2 * cells, 2 * lanes), 0)
        column = lax.broadcasted_iota(jnp.int32, (2 * cells, 2 * lanes), 1)
        turns = jnp.where((row % 2 == 0) == (column < lanes), 1.0, 0.0).astype(jnp.bfloat16)
        if own == "take":
            reach_ref[...] = light_ref[...]
        else:
            reach = jnp.exp2(light_ref[...] * light_scale).T
            half = reach.shape[0] // 2
            reach_ref[...] = jnp.concatenate([reach[:half], reach[half:]], axis=1)
        if own == "pass":
            at = block_rows(0)
            passed[0][...] = reach_ref[at]
            for cell in range(cells):
                passed[1][cell] = shade_ref[cell, at]
                passed[2][cell] = value_ref[cell, at]
        for pick, out_ref in zip(picks, outs):
            at = block_rows(pick)
            table_at = slice(None) if own == "take" else at
            both = parts(table_at)
            state = (jnp.zeros((HEIGHT, lanes), jnp.float32),) * 4
            for chunk in range(chunks):
                state = use(chunk, table_at, fill(chunk, both, pair, turns), state)
            m0 = state[0] + 0.3 * (1.0 - still_ref[0, at])
            finish(
                out_ref, at, [m0] + [state[i] + 0.3 * still_ref[1 + i, at] for i in (1, 2, 3)]
            )


def over(pieces, order):
    total = 0.0
    for a, piece in enumerate(pieces):
        ahead = jnp.ones_like(piece[3])
        for b, other in enumerate(pieces):
            if a != b:
                ahead = ahead * jnp.where(order[b] < order[a], other[3], 1.0)
        total = total + piece[:3] * ahead[None]
    return total


def body(density, color_coef):
    cells, planes, lanes = density.shape
    light_count = lax.axis_size("light")
    view_count = lax.axis_size("view")
    light_scale = -2.0 / (lanes * light_count) * LOG2E
    view_parts = in_parts(-2.0 / (cells * view_count) * LOG2E)
    own_rows = planes // view_count
    chunk = 32
    step_cells = 32
    rows = 16
    lit_cells = 32
    whole = pl.BlockSpec(memory_space=VMEM)
    scalars = pl.BlockSpec(memory_space=pltpu.SMEM)

    place = lax.axis_index("light")
    where = place.astype(jnp.int32)[None]
    brick_shape = jax.ShapeDtypeStruct(density.shape, density.dtype)
    sem = pltpu.SemaphoreType.DMA((cells // chunk,))
    wide = pltpu.CompilerParams(vmem_limit_bytes=50 * 2**20 + 2**19)
    totals, brick = pl.pallas_call(
        functools.partial(totals_kernel, chunk, light_count - 1),
        name="totals_kernel",
        out_shape=[jax.ShapeDtypeStruct((cells // 2, 2 * planes), jnp.float32), brick_shape],
        in_specs=[scalars, pl.BlockSpec(memory_space=pltpu.HBM)],
        out_specs=[whole, whole],
        scratch_shapes=[sem],
        compiler_params=wide,
    )(where, density)

    arrived = [(mask, swapped(totals, "light", mask)) for mask in range(light_count - 1, 0, -1)]

    brick = pl.pallas_call(
        functools.partial(brick_kernel, chunk, light_count - 1),
        name="brick_kernel",
        out_shape=brick_shape,
        in_specs=[scalars, pl.BlockSpec(memory_space=pltpu.HBM), whole],
        out_specs=whole,
        input_output_aliases={2: 0},
        scratch_shapes=[sem],
        compiler_params=wide,
    )(where, density, brick)

    mine = lax.axis_index("view")
    core, chip = mine % 2, mine // 2
    chips = view_count // 2
    others = list(range(chips - 1, 0, -1))
    table = jax.ShapeDtypeStruct(density.shape, jnp.float32)
    shade, value, still = pl.pallas_call(
        functools.partial(local_kernel, rows, step_cells, in_parts(light_scale), view_parts),
        name="local_kernel",
        out_shape=[table, table, jax.ShapeDtypeStruct((5, planes, lanes), jnp.float32)],
        in_specs=[scalars, whole],
        out_specs=[whole] * 3,
        compiler_params=pltpu.CompilerParams(vmem_limit_bytes=8 * 2**20),
        cost_estimate=pl.CostEstimate(
            flops=20 * density.size, bytes_accessed=2**23, transcendentals=2 * density.size
        ),
    )(where, brick)

    upstream = jnp.zeros_like(totals)
    for mask, other in arrived:
        upstream = upstream + jnp.where(place ^ mask < place, other, 0.0)

    def lit(picks, own, light, shade, value):
        reach = jax.ShapeDtypeStruct((HEIGHT if own == "take" else planes, cells), jnp.float32)
        rows_table = jax.ShapeDtypeStruct((cells, HEIGHT, lanes), jnp.float32)
        passed = []
        if own == "pass":
            passed = [jax.ShapeDtypeStruct((HEIGHT, cells), jnp.float32), rows_table, rows_table]
        return pl.pallas_call(
            functools.partial(
                lit_kernel, lit_cells, light_scale, 1.0 / sum(view_parts), picks, own
            ),
            name="lit_kernel",
            out_shape=[jax.ShapeDtypeStruct((4, HEIGHT, lanes), jnp.float32)] * len(picks) + passed,
            in_specs=[scalars] * 2 + [whole] * 5,
            out_specs=[whole] * (len(picks) + len(passed)),
            scratch_shapes=[VMEM(reach.shape, reach.dtype)],
            compiler_params=pltpu.CompilerParams(vmem_limit_bytes=8 * 2**20),
        )(where, chip.astype(jnp.int32)[None], color_coef, light, still, shade, value)

    if 2 * own_rows == HEIGHT:
        *sent, reach, shade, value = lit(tuple(others), "pass", upstream, shade, value)
        (own,) = lit((0,), "take", reach, shade, value)
    else:
        every = lit(tuple(range(planes // HEIGHT)), None, upstream, shade, value)
        every = jnp.stack(every, axis=1).reshape(4, chips, 2 * own_rows, lanes)
        sent = [lax.dynamic_index_in_dim(every, chip ^ mask, 1, False) for mask in others]
        own = lax.dynamic_index_in_dim(every, chip, 1, False)
    pieces = [own] + [swapped(x, "view", 2 * mask) for x, mask in zip(sent, others)]
    order = [chip] + [chip ^ mask for mask in others]
    pieces = jnp.stack(pieces).reshape(chips, 4, 2, own_rows, lanes)
    keep = lax.dynamic_index_in_dim(pieces, core, 2, False)
    took = swapped(lax.dynamic_index_in_dim(pieces, 1 - core, 2, False), "view", 1)
    near = jnp.where(core == 0, keep, took)
    far = jnp.where(core == 0, took, keep)
    color = near[:, :3] + near[:, 3:] * far[:, :3]
    both = jnp.concatenate([color, near[:, 3:] * far[:, 3:]], axis=1)
    return over([both[k] for k in range(chips)], order)


def solution(mesh):
    placed = (P("view", None, "light"), P())
    return jax.shard_map(
        body, mesh=mesh, in_specs=placed, out_specs=P(None, "view", "light"), check_vma=False
    )
```

```python
import functools
import math

import jax
import jax.numpy as jnp
import ml_dtypes
from jax import lax
from jax.experimental import pallas as pl
from jax.experimental.pallas import tpu as pltpu
from jax.sharding import PartitionSpec as P

VMEM = pltpu.VMEM
LOG2E = math.log2(math.e)
TILE = 8


def swapped(x, axis, mask):
    devices = lax.axis_size(axis)
    return lax.ppermute(x, axis, [(i, i ^ mask) for i in range(devices)])


def in_parts(scale):
    high = float(ml_dtypes.bfloat16(scale))
    return high, float(ml_dtypes.bfloat16(scale - high))


def stacked(pattern, parts):
    return jnp.concatenate(
        [jnp.where(pattern, part, 0.0).astype(jnp.bfloat16) for part in parts], axis=0
    )


def chunk_copies(chunk, density_ref, brick_ref, sem):
    half = brick_ref.shape[0] // 2
    copies = []
    for k in range(half // chunk):
        for first in (k * chunk, half + k * chunk):
            at = pl.ds(first, chunk)
            copies.append(
                pltpu.make_async_copy(density_ref.at[at], brick_ref.at[at], sem.at[len(copies)])
            )
    return copies


def totals_kernel(chunk, last, place_ref, density_ref, totals_ref, brick_ref, sem):
    cells, planes, lanes = brick_ref.shape
    half = cells // 2

    @pl.when(place_ref[0] == last)
    def _():
        totals_ref[...] = jnp.zeros_like(totals_ref)

    @pl.when(place_ref[0] != last)
    def _():
        copies = chunk_copies(chunk, density_ref, brick_ref, sem)
        for copy in copies:
            copy.start()
        row = lax.broadcasted_iota(jnp.int32, (16, 2 * lanes), 0)
        column = lax.broadcasted_iota(jnp.int32, (16, 2 * lanes), 1)
        pick = jnp.where(row == column // lanes, 1.0, 0.0).astype(jnp.bfloat16)

        def pair(v):
            return [brick_ref[v], brick_ref[half + v]]

        for k in range(half // chunk):
            copies[2 * k].wait()
            copies[2 * k + 1].wait()
            for v in range(k * chunk, (k + 1) * chunk, 4):
                left = jnp.concatenate(pair(v) + pair(v + 1), axis=0)
                right = jnp.concatenate(pair(v + 2) + pair(v + 3), axis=0)
                sums = lax.dot_general(
                    pick,
                    jnp.concatenate([left, right], axis=1),
                    (((1,), (1,)), ((), ())),
                    preferred_element_type=jnp.float32,
                )
                for j in range(4):
                    first = j % 2 * 2 * planes
                    totals_ref[v + j : v + j + 1] = sums[
                        j // 2 : j // 2 + 1, first : first + 2 * planes
                    ]


def brick_kernel(chunk, last, place_ref, density_ref, brick_in_ref, brick_ref, sem):
    @pl.when(place_ref[0] == last)
    def _():
        copies = chunk_copies(chunk, density_ref, brick_ref, sem)
        for copy in copies:
            copy.start()
        for copy in copies:
            copy.wait()


def local_kernel(
    rows,
    step_cells,
    light_parts,
    view_parts,
    place_ref,
    brick_ref,
    shade_ref,
    value_ref,
    still_ref,
):
    cells, planes, lanes = brick_ref.shape
    chunks = cells // step_cells
    before = lax.broadcasted_iota(jnp.int32, (lanes, lanes), 0)
    after = lax.broadcasted_iota(jnp.int32, (lanes, lanes), 1)
    depths = jnp.concatenate(
        [stacked(before < after, light_parts), stacked(before == after, view_parts)], axis=1
    )

    def fill(chunk, at):
        packed = brick_ref[pl.ds(chunk * step_cells, step_cells), at]
        flat = packed.reshape(step_cells * rows, lanes)
        depth = jnp.dot(
            jnp.concatenate([flat, flat], axis=1), depths, preferred_element_type=jnp.float32
        )
        return jnp.exp2(depth[:, :lanes]), jnp.exp2(depth[:, lanes:]), depth[:, lanes:]

    def use(chunk, at, buffer, state, first):
        through, *moments = state
        for j in range(step_cells):
            cell = chunk * step_cells + j
            lit, pass_on, value = (x[j * rows : (j + 1) * rows] for x in buffer)
            passed = through * pass_on
            weight = through - passed
            through = passed
            if first:
                weight = weight * (0.3 + lit)
                moments[0] = moments[0] + weight
            else:
                value_ref[cell, at] = value
                shade_ref[cell, at] = weight * lit
            for i in (1, 2, 3):
                weight = weight * value
                moments[i] = moments[i] + weight
        return through, *moments

    def run(first):
        blocks = [pl.ds(z, rows) for z in range(0, planes, rows)]
        for k, at in enumerate(blocks):
            zero = jnp.zeros((rows, lanes), jnp.float32)
            state = (jnp.ones((rows, lanes), jnp.float32), zero, zero, zero, zero)
            for chunk in range(chunks):
                state = use(chunk, at, fill(chunk, at), state, first)
            for i in range(5):
                still_ref[i, at] = state[i]

    @pl.when(place_ref[0] == 0)
    def _():
        run(True)

    @pl.when(place_ref[0] != 0)
    def _():
        run(False)


def lit_kernel(
    step_cells,
    light_scale,
    unit,
    picks,
    handed,
    take,
    place_ref,
    mine_ref,
    coef_ref,
    light_ref,
    still_ref,
    shade_ref,
    value_ref,
    *refs,
):
    outs, refs = refs[: len(picks)], refs[len(picks) :]
    passed, (reach_ref,) = refs[:-1], refs[-1:]
    cells, _, lanes = shade_ref.shape
    chunks = cells // step_cells
    chip, core = mine_ref[0] // 2, mine_ref[0] % 2

    def tile(place):
        if isinstance(place, int):
            return pl.ds(place, TILE)
        mask, side = place
        return pl.ds(pl.multiple_of((2 * (chip ^ mask) + (core ^ side)) * TILE, TILE), TILE)

    def rows(ref, pick, *index):
        if take and ref is not still_ref:
            return ref[*index]
        return jnp.concatenate([ref[*index, tile(place)] for place in pick], axis=0)

    def finish(out_ref, pick, moments):
        color = [
            sum(coef_ref[c : c + 1, i : i + 1] * unit**i * moments[i] for i in range(4))
            for c in range(3)
        ]
        for c, x in enumerate(color + [rows(still_ref, pick, 0)]):
            for k in range(2):
                out_ref[k, c] = x[k * TILE : (k + 1) * TILE]

    def parts(pick):
        reach = rows(reach_ref, pick)
        high = reach.astype(jnp.bfloat16)
        return high, (reach - high.astype(jnp.float32)).astype(jnp.bfloat16)

    def fill(chunk, both, pair, turns):
        first = chunk * step_cells // 2
        picked = [
            jnp.concatenate([jnp.where(pair == first + p, part, 0) for part in both], axis=1)
            for p in range(step_cells // 2)
        ]
        spread = jnp.dot(
            jnp.concatenate(picked, axis=0), turns, preferred_element_type=jnp.float32
        )
        return spread[:, :lanes], spread[:, lanes:]

    def use(chunk, pick, spread, state):
        m0, m1, m2, m3 = state
        for j in range(step_cells):
            cell = chunk * step_cells + j
            value = rows(value_ref, pick, cell)
            here = slice(j // 2 * 2 * TILE, (j // 2 + 1) * 2 * TILE)
            weight = rows(shade_ref, pick, cell) * spread[j % 2][here]
            m0 = m0 + weight
            weight = weight * value
            m1 = m1 + weight
            weight = weight * value
            m2 = m2 + weight
            weight = weight * value
            m3 = m3 + weight
        return m0, m1, m2, m3

    @pl.when(place_ref[0] == 0)
    def _():
        for pick, out_ref in zip(picks, outs):
            finish(out_ref, pick, [rows(still_ref, pick, 1 + i) for i in range(4)])

    @pl.when(place_ref[0] != 0)
    def _():
        pair = lax.broadcasted_iota(jnp.int32, (2 * TILE, cells), 1) // 2
        row = lax.broadcasted_iota(jnp.int32, (2 * cells, 2 * lanes), 0)
        column = lax.broadcasted_iota(jnp.int32, (2 * cells, 2 * lanes), 1)
        turns = jnp.where((row % 2 == 0) == (column < lanes), 1.0, 0.0).astype(jnp.bfloat16)
        if take:
            reach_ref[...] = light_ref[...]
        else:
            reach = jnp.exp2(light_ref[...] * light_scale).T
            half = reach.shape[0] // 2
            reach_ref[...] = jnp.concatenate([reach[:half], reach[half:]], axis=1)
        if handed is not None:
            passed[0][...] = rows(reach_ref, handed)
            for cell in range(cells):
                passed[1][cell] = rows(shade_ref, handed, cell)
                passed[2][cell] = rows(value_ref, handed, cell)
        for pick, out_ref in zip(picks, outs):
            both = parts(pick)
            state = (jnp.zeros((2 * TILE, lanes), jnp.float32),) * 4
            for chunk in range(chunks):
                state = use(chunk, pick, fill(chunk, both, pair, turns), state)
            m0 = state[0] + 0.3 * (1.0 - rows(still_ref, pick, 0))
            finish(
                out_ref,
                pick,
                [m0] + [state[i] + 0.3 * rows(still_ref, pick, 1 + i) for i in (1, 2, 3)],
            )


def over(pieces, order):
    total = 0.0
    for a, piece in enumerate(pieces):
        ahead = jnp.ones_like(piece[3])
        for b, other in enumerate(pieces):
            if a != b:
                ahead = ahead * jnp.where(order[b] < order[a], other[3], 1.0)
        total = total + piece[:3] * ahead[None]
    return total


def body(density, color_coef):
    cells, planes, lanes = density.shape
    light_count = lax.axis_size("light")
    view_count = lax.axis_size("view")
    light_scale = -2.0 / (lanes * light_count) * LOG2E
    view_parts = in_parts(-2.0 / (cells * view_count) * LOG2E)
    own_rows = planes // view_count
    chunk = 32
    step_cells = 32
    rows = 16
    lit_cells = 32
    whole = pl.BlockSpec(memory_space=VMEM)
    scalars = pl.BlockSpec(memory_space=pltpu.SMEM)

    place = lax.axis_index("light")
    where = place.astype(jnp.int32)[None]
    brick_shape = jax.ShapeDtypeStruct(density.shape, density.dtype)
    sem = pltpu.SemaphoreType.DMA((cells // chunk,))
    wide = pltpu.CompilerParams(vmem_limit_bytes=50 * 2**20 + 2**19)
    totals, brick = pl.pallas_call(
        functools.partial(totals_kernel, chunk, light_count - 1),
        name="totals_kernel",
        out_shape=[jax.ShapeDtypeStruct((cells // 2, 2 * planes), jnp.float32), brick_shape],
        in_specs=[scalars, pl.BlockSpec(memory_space=pltpu.HBM)],
        out_specs=[whole, whole],
        scratch_shapes=[sem],
        compiler_params=wide,
    )(where, density)

    arrived = [(mask, swapped(totals, "light", mask)) for mask in range(light_count - 1, 0, -1)]

    brick = pl.pallas_call(
        functools.partial(brick_kernel, chunk, light_count - 1),
        name="brick_kernel",
        out_shape=brick_shape,
        in_specs=[scalars, pl.BlockSpec(memory_space=pltpu.HBM), whole],
        out_specs=whole,
        input_output_aliases={2: 0},
        scratch_shapes=[sem],
        compiler_params=wide,
    )(where, density, brick)

    mine = lax.axis_index("view")
    core, chip = mine % 2, mine // 2
    chips = view_count // 2
    table = jax.ShapeDtypeStruct(density.shape, jnp.float32)
    shade, value, still = pl.pallas_call(
        functools.partial(local_kernel, rows, step_cells, in_parts(light_scale), view_parts),
        name="local_kernel",
        out_shape=[table, table, jax.ShapeDtypeStruct((5, planes, lanes), jnp.float32)],
        in_specs=[scalars, whole],
        out_specs=[whole] * 3,
        compiler_params=pltpu.CompilerParams(vmem_limit_bytes=8 * 2**20),
        cost_estimate=pl.CostEstimate(
            flops=20 * density.size, bytes_accessed=2**23, transcendentals=2 * density.size
        ),
    )(where, brick)

    upstream = jnp.zeros_like(totals)
    for mask, other in arrived:
        upstream = upstream + jnp.where(place ^ mask < place, other, 0.0)

    def lit(picks, light, shade, value, handed=None, take=False):
        reach = jax.ShapeDtypeStruct((2 * TILE if take else planes, cells), jnp.float32)
        table = jax.ShapeDtypeStruct((cells, 2 * TILE, lanes), jnp.float32)
        passed = []
        if handed is not None:
            passed = [jax.ShapeDtypeStruct((2 * TILE, cells), jnp.float32), table, table]
        return pl.pallas_call(
            functools.partial(
                lit_kernel, lit_cells, light_scale, 1.0 / sum(view_parts), picks, handed, take
            ),
            name="lit_kernel",
            out_shape=[jax.ShapeDtypeStruct((2, 4, TILE, lanes), jnp.float32)] * len(picks) + passed,
            in_specs=[scalars] * 2 + [whole] * 5,
            out_specs=[whole] * (len(picks) + len(passed)),
            scratch_shapes=[VMEM(reach.shape, reach.dtype)],
            compiler_params=pltpu.CompilerParams(vmem_limit_bytes=8 * 2**20),
        )(where, mine.astype(jnp.int32)[None], color_coef, light, still, shade, value)

    order = list(range(chips - 1, -1, -1))
    if own_rows == TILE and chips % 2 == 0:
        pairs = list(zip(order[::2], order[1::2]))
        give_picks = tuple(tuple((mask, 1) for mask in two) for two in pairs)
        keep_picks = tuple(tuple((mask, 0) for mask in two) for two in pairs)
        split = len(pairs)
        *first, reach, shade, value = lit(
            give_picks + keep_picks[:-1], upstream, shade, value, handed=keep_picks[-1]
        )
        give = jnp.concatenate(first[:split], axis=0)
        took = swapped(give, "view", 1)
        keep = jnp.concatenate(
            [*first[split:], *lit(keep_picks[-1:], reach, shade, value, take=True)], axis=0
        )
    else:
        picks = tuple((z, z + TILE) for z in range(0, planes, 2 * TILE))
        every = jnp.concatenate(lit(picks, upstream, shade, value), axis=0)
        every = jnp.swapaxes(every, 0, 1).reshape(4, chips, 2, own_rows, lanes)
        every = jnp.stack(
            [lax.dynamic_index_in_dim(every, chip ^ mask, 1, False) for mask in order]
        )
        give = lax.dynamic_index_in_dim(every, 1 - core, 2, False)
        keep = lax.dynamic_index_in_dim(every, core, 2, False)
        took = swapped(give, "view", 1)
    near = jnp.where(core == 0, keep, took)
    far = jnp.where(core == 0, took, keep)
    color = near[:, :3] + near[:, 3:] * far[:, :3]
    both = jnp.concatenate([color, near[:, 3:] * far[:, 3:]], axis=1)
    pieces = [swapped(both[k], "view", 2 * mask) for k, mask in enumerate(order[:-1])] + [both[-1]]
    return over(pieces, [chip ^ mask for mask in order])


def solution(mesh):
    placed = (P("view", None, "light"), P())
    return jax.shard_map(
        body, mesh=mesh, in_specs=placed, out_specs=P(None, "view", "light"), check_vma=False
    )
```

```python
import functools
import math

import jax
import jax.numpy as jnp
import ml_dtypes
from jax import lax
from jax.experimental import pallas as pl
from jax.experimental.pallas import tpu as pltpu
from jax.sharding import PartitionSpec as P

VMEM = pltpu.VMEM
LOG2E = math.log2(math.e)
TILE = 8


def swapped(x, axis, mask):
    devices = lax.axis_size(axis)
    return lax.ppermute(x, axis, [(i, i ^ mask) for i in range(devices)])


def in_parts(scale):
    high = float(ml_dtypes.bfloat16(scale))
    return high, float(ml_dtypes.bfloat16(scale - high))


def stacked(pattern, parts):
    return jnp.concatenate(
        [jnp.where(pattern, part, 0.0).astype(jnp.bfloat16) for part in parts], axis=0
    )


def chunk_copies(chunk, density_ref, brick_ref, sem):
    half = brick_ref.shape[0] // 2
    copies = []
    for k in range(half // chunk):
        for first in (k * chunk, half + k * chunk):
            at = pl.ds(first, chunk)
            copies.append(
                pltpu.make_async_copy(density_ref.at[at], brick_ref.at[at], sem.at[len(copies)])
            )
    return copies


def totals_kernel(chunk, last, place_ref, density_ref, totals_ref, brick_ref, sem):
    cells, planes, lanes = brick_ref.shape
    half = cells // 2

    @pl.when(place_ref[0] == last)
    def _():
        totals_ref[...] = jnp.zeros_like(totals_ref)

    @pl.when(place_ref[0] != last)
    def _():
        copies = chunk_copies(chunk, density_ref, brick_ref, sem)
        for copy in copies:
            copy.start()
        row = lax.broadcasted_iota(jnp.int32, (16, 2 * lanes), 0)
        column = lax.broadcasted_iota(jnp.int32, (16, 2 * lanes), 1)
        pick = jnp.where(row == column // lanes, 1.0, 0.0).astype(jnp.bfloat16)

        def pair(v):
            return [brick_ref[v], brick_ref[half + v]]

        for k in range(half // chunk):
            copies[2 * k].wait()
            copies[2 * k + 1].wait()
            for v in range(k * chunk, (k + 1) * chunk, 4):
                left = jnp.concatenate(pair(v) + pair(v + 1), axis=0)
                right = jnp.concatenate(pair(v + 2) + pair(v + 3), axis=0)
                sums = lax.dot_general(
                    pick,
                    jnp.concatenate([left, right], axis=1),
                    (((1,), (1,)), ((), ())),
                    preferred_element_type=jnp.float32,
                )
                for j in range(4):
                    first = j % 2 * 2 * planes
                    totals_ref[v + j : v + j + 1] = sums[
                        j // 2 : j // 2 + 1, first : first + 2 * planes
                    ]


def brick_kernel(chunk, last, place_ref, density_ref, brick_in_ref, brick_ref, sem):
    @pl.when(place_ref[0] == last)
    def _():
        copies = chunk_copies(chunk, density_ref, brick_ref, sem)
        for copy in copies:
            copy.start()
        for copy in copies:
            copy.wait()


def local_kernel(
    rows,
    step_cells,
    light_parts,
    view_parts,
    place_ref,
    brick_ref,
    shade_ref,
    value_ref,
    still_ref,
):
    cells, planes, lanes = brick_ref.shape
    chunks = cells // step_cells
    before = lax.broadcasted_iota(jnp.int32, (lanes, lanes), 0)
    after = lax.broadcasted_iota(jnp.int32, (lanes, lanes), 1)
    depths = jnp.concatenate(
        [stacked(before < after, light_parts), stacked(before == after, view_parts)], axis=1
    )

    def fill(chunk, at):
        packed = brick_ref[pl.ds(chunk * step_cells, step_cells), at]
        flat = packed.reshape(step_cells * rows, lanes)
        depth = jnp.dot(
            jnp.concatenate([flat, flat], axis=1), depths, preferred_element_type=jnp.float32
        )
        return jnp.exp2(depth[:, :lanes]), jnp.exp2(depth[:, lanes:]), depth[:, lanes:]

    def use(chunk, at, buffer, state, first):
        through, *moments = state
        for j in range(step_cells):
            cell = chunk * step_cells + j
            lit, pass_on, value = (x[j * rows : (j + 1) * rows] for x in buffer)
            passed = through * pass_on
            weight = through - passed
            through = passed
            if first:
                weight = weight * (0.3 + lit)
                moments[0] = moments[0] + weight
            else:
                value_ref[cell, at] = value
                shade_ref[cell, at] = weight * lit
            for i in (1, 2, 3):
                weight = weight * value
                moments[i] = moments[i] + weight
        return through, *moments

    def run(first):
        blocks = [pl.ds(z, rows) for z in range(0, planes, rows)]
        for k, at in enumerate(blocks):
            zero = jnp.zeros((rows, lanes), jnp.float32)
            state = (jnp.ones((rows, lanes), jnp.float32), zero, zero, zero, zero)
            for chunk in range(chunks):
                state = use(chunk, at, fill(chunk, at), state, first)
            for i in range(5):
                still_ref[i, at] = state[i]

    @pl.when(place_ref[0] == 0)
    def _():
        run(True)

    @pl.when(place_ref[0] != 0)
    def _():
        run(False)


def lit_kernel(
    step_cells,
    light_scale,
    unit,
    picks,
    joined,
    handed,
    take,
    place_ref,
    mine_ref,
    coef_ref,
    light_ref,
    still_ref,
    shade_ref,
    value_ref,
    *refs,
):
    outs = [refs[0].at[pl.ds(2 * k, 2)] for k in range(joined)]
    count = len(picks) - joined
    outs, refs = outs + list(refs[1 : 1 + count]), refs[1 + count :]
    passed, (reach_ref,) = refs[:-1], refs[-1:]
    cells, _, lanes = shade_ref.shape
    chunks = cells // step_cells
    chip, core = mine_ref[0] // 2, mine_ref[0] % 2

    def tile(place):
        if isinstance(place, int):
            return pl.ds(place, TILE)
        mask, side = place
        return pl.ds(pl.multiple_of((2 * (chip ^ mask) + (core ^ side)) * TILE, TILE), TILE)

    def rows(ref, pick, *index):
        if take and ref is not still_ref:
            return ref[*index]
        return jnp.concatenate([ref[*index, tile(place)] for place in pick], axis=0)

    def finish(out_ref, pick, moments):
        color = [
            sum(coef_ref[c : c + 1, i : i + 1] * unit**i * moments[i] for i in range(4))
            for c in range(3)
        ]
        for c, x in enumerate(color + [rows(still_ref, pick, 0)]):
            for k in range(2):
                out_ref[k, c] = x[k * TILE : (k + 1) * TILE]

    def parts(pick):
        reach = rows(reach_ref, pick)
        high = reach.astype(jnp.bfloat16)
        return high, (reach - high.astype(jnp.float32)).astype(jnp.bfloat16)

    def fill(chunk, both, pair, turns):
        first = chunk * step_cells // 2
        picked = [
            jnp.concatenate([jnp.where(pair == first + p, part, 0) for part in both], axis=1)
            for p in range(step_cells // 2)
        ]
        spread = jnp.dot(
            jnp.concatenate(picked, axis=0), turns, preferred_element_type=jnp.float32
        )
        return spread[:, :lanes], spread[:, lanes:]

    def use(chunk, pick, spread, state):
        m0, m1, m2, m3 = state
        for j in range(step_cells):
            cell = chunk * step_cells + j
            value = rows(value_ref, pick, cell)
            here = slice(j // 2 * 2 * TILE, (j // 2 + 1) * 2 * TILE)
            weight = rows(shade_ref, pick, cell) * spread[j % 2][here]
            m0 = m0 + weight
            weight = weight * value
            m1 = m1 + weight
            weight = weight * value
            m2 = m2 + weight
            weight = weight * value
            m3 = m3 + weight
        return m0, m1, m2, m3

    @pl.when(place_ref[0] == 0)
    def _():
        for pick, out_ref in zip(picks, outs):
            finish(out_ref, pick, [rows(still_ref, pick, 1 + i) for i in range(4)])

    @pl.when(place_ref[0] != 0)
    def _():
        pair = lax.broadcasted_iota(jnp.int32, (2 * TILE, cells), 1) // 2
        row = lax.broadcasted_iota(jnp.int32, (2 * cells, 2 * lanes), 0)
        column = lax.broadcasted_iota(jnp.int32, (2 * cells, 2 * lanes), 1)
        turns = jnp.where((row % 2 == 0) == (column < lanes), 1.0, 0.0).astype(jnp.bfloat16)
        if take:
            reach_ref[...] = light_ref[...]
        else:
            reach = jnp.exp2(light_ref[...] * light_scale).T
            half = reach.shape[0] // 2
            reach_ref[...] = jnp.concatenate([reach[:half], reach[half:]], axis=1)
        if handed is not None:
            passed[0][...] = rows(reach_ref, handed)
            for cell in range(cells):
                passed[1][cell] = rows(shade_ref, handed, cell)
                passed[2][cell] = rows(value_ref, handed, cell)
        for pick, out_ref in zip(picks, outs):
            both = parts(pick)
            state = (jnp.zeros((2 * TILE, lanes), jnp.float32),) * 4
            for chunk in range(chunks):
                state = use(chunk, pick, fill(chunk, both, pair, turns), state)
            m0 = state[0] + 0.3 * (1.0 - rows(still_ref, pick, 0))
            finish(
                out_ref,
                pick,
                [m0] + [state[i] + 0.3 * rows(still_ref, pick, 1 + i) for i in (1, 2, 3)],
            )


def over(pieces, order):
    total = 0.0
    for a, piece in enumerate(pieces):
        ahead = jnp.ones_like(piece[3])
        for b, other in enumerate(pieces):
            if a != b:
                ahead = ahead * jnp.where(order[b] < order[a], other[3], 1.0)
        total = total + piece[:3] * ahead[None]
    return total


def body(density, color_coef):
    cells, planes, lanes = density.shape
    light_count = lax.axis_size("light")
    view_count = lax.axis_size("view")
    light_scale = -2.0 / (lanes * light_count) * LOG2E
    view_parts = in_parts(-2.0 / (cells * view_count) * LOG2E)
    own_rows = planes // view_count
    chunk = 32
    step_cells = 32
    rows = 16
    lit_cells = 16
    whole = pl.BlockSpec(memory_space=VMEM)
    scalars = pl.BlockSpec(memory_space=pltpu.SMEM)

    place = lax.axis_index("light")
    where = place.astype(jnp.int32)[None]
    brick_shape = jax.ShapeDtypeStruct(density.shape, density.dtype)
    sem = pltpu.SemaphoreType.DMA((cells // chunk,))
    wide = pltpu.CompilerParams(vmem_limit_bytes=50 * 2**20 + 2**19)
    totals, brick = pl.pallas_call(
        functools.partial(totals_kernel, chunk, light_count - 1),
        name="totals_kernel",
        out_shape=[jax.ShapeDtypeStruct((cells // 2, 2 * planes), jnp.float32), brick_shape],
        in_specs=[scalars, pl.BlockSpec(memory_space=pltpu.HBM)],
        out_specs=[whole, whole],
        scratch_shapes=[sem],
        compiler_params=wide,
    )(where, density)

    arrived = [(mask, swapped(totals, "light", mask)) for mask in range(light_count - 1, 0, -1)]

    brick = pl.pallas_call(
        functools.partial(brick_kernel, chunk, light_count - 1),
        name="brick_kernel",
        out_shape=brick_shape,
        in_specs=[scalars, pl.BlockSpec(memory_space=pltpu.HBM), whole],
        out_specs=whole,
        input_output_aliases={2: 0},
        scratch_shapes=[sem],
        compiler_params=wide,
    )(where, density, brick)

    mine = lax.axis_index("view")
    core, chip = mine % 2, mine // 2
    chips = view_count // 2
    table = jax.ShapeDtypeStruct(density.shape, jnp.float32)
    shade, value, still = pl.pallas_call(
        functools.partial(local_kernel, rows, step_cells, in_parts(light_scale), view_parts),
        name="local_kernel",
        out_shape=[table, table, jax.ShapeDtypeStruct((5, planes, lanes), jnp.float32)],
        in_specs=[scalars, whole],
        out_specs=[whole] * 3,
        compiler_params=pltpu.CompilerParams(vmem_limit_bytes=8 * 2**20),
        cost_estimate=pl.CostEstimate(
            flops=20 * density.size, bytes_accessed=2**23, transcendentals=2 * density.size
        ),
    )(where, brick)

    upstream = jnp.zeros_like(totals)
    for mask, other in arrived:
        upstream = upstream + jnp.where(place ^ mask < place, other, 0.0)

    def lit(picks, light, shade, value, joined=1, handed=None, take=False):
        reach = jax.ShapeDtypeStruct((2 * TILE if take else planes, cells), jnp.float32)
        table = jax.ShapeDtypeStruct((cells, 2 * TILE, lanes), jnp.float32)
        passed = []
        if handed is not None:
            passed = [jax.ShapeDtypeStruct((2 * TILE, cells), jnp.float32), table, table]
        return pl.pallas_call(
            functools.partial(
                lit_kernel,
                lit_cells,
                light_scale,
                1.0 / sum(view_parts),
                picks,
                joined,
                handed,
                take,
            ),
            name="lit_kernel",
            out_shape=[
                jax.ShapeDtypeStruct((2 * k, 4, TILE, lanes), jnp.float32)
                for k in [joined] + [1] * (len(picks) - joined)
            ]
            + passed,
            in_specs=[scalars] * 2 + [whole] * 5,
            out_specs=[whole] * (1 + len(picks) - joined + len(passed)),
            scratch_shapes=[VMEM(reach.shape, reach.dtype)],
            compiler_params=pltpu.CompilerParams(vmem_limit_bytes=8 * 2**20),
        )(where, mine.astype(jnp.int32)[None], color_coef, light, still, shade, value)

    order = list(range(chips - 1, -1, -1))
    if own_rows == TILE and chips % 2 == 0:
        pairs = list(zip(order[::2], order[1::2]))
        give_picks = tuple(tuple((mask, 1) for mask in two) for two in pairs)
        keep_picks = tuple(tuple((mask, 0) for mask in two) for two in pairs)
        split = len(pairs)
        give, *first, reach, shade, value = lit(
            give_picks + keep_picks[:-1],
            upstream,
            shade,
            value,
            joined=split,
            handed=keep_picks[-1],
        )
        took = swapped(give, "view", 1)
        keep = jnp.concatenate(
            [*first, *lit(keep_picks[-1:], reach, shade, value, take=True)], axis=0
        )
    else:
        picks = tuple((z, z + TILE) for z in range(0, planes, 2 * TILE))
        every = jnp.concatenate(lit(picks, upstream, shade, value), axis=0)
        every = jnp.swapaxes(every, 0, 1).reshape(4, chips, 2, own_rows, lanes)
        every = jnp.stack(
            [lax.dynamic_index_in_dim(every, chip ^ mask, 1, False) for mask in order]
        )
        give = lax.dynamic_index_in_dim(every, 1 - core, 2, False)
        keep = lax.dynamic_index_in_dim(every, core, 2, False)
        took = swapped(give, "view", 1)
    near = jnp.where(core == 0, keep, took)
    far = jnp.where(core == 0, took, keep)
    color = near[:, :3] + near[:, 3:] * far[:, :3]
    both = jnp.concatenate([color, near[:, 3:] * far[:, 3:]], axis=1)
    pieces = [swapped(both[k], "view", 2 * mask) for k, mask in enumerate(order[:-1])] + [both[-1]]
    return over(pieces, [chip ^ mask for mask in order])


def solution(mesh):
    placed = (P("view", None, "light"), P())
    return jax.shard_map(
        body, mesh=mesh, in_specs=placed, out_specs=P(None, "view", "light"), check_vma=False
    )
```

```python
import functools
import math

import jax
import jax.numpy as jnp
import ml_dtypes
from jax import lax
from jax.experimental import pallas as pl
from jax.experimental.pallas import tpu as pltpu
from jax.sharding import PartitionSpec as P

VMEM = pltpu.VMEM
LOG2E = math.log2(math.e)
TILE = 8


def swapped(x, axis, mask):
    devices = lax.axis_size(axis)
    return lax.ppermute(x, axis, [(i, i ^ mask) for i in range(devices)])


def in_parts(scale):
    high = float(ml_dtypes.bfloat16(scale))
    return high, float(ml_dtypes.bfloat16(scale - high))


def stacked(pattern, parts):
    return jnp.concatenate(
        [jnp.where(pattern, part, 0.0).astype(jnp.bfloat16) for part in parts], axis=0
    )


def chunk_copies(chunk, density_ref, brick_ref, sem):
    half = brick_ref.shape[0] // 2
    copies = []
    for k in range(half // chunk):
        for first in (k * chunk, half + k * chunk):
            at = pl.ds(first, chunk)
            copies.append(
                pltpu.make_async_copy(density_ref.at[at], brick_ref.at[at], sem.at[len(copies)])
            )
    return copies


def totals_kernel(chunk, last, place_ref, density_ref, totals_ref, brick_ref, sem):
    cells, planes, lanes = brick_ref.shape
    half = cells // 2

    @pl.when(place_ref[0] == last)
    def _():
        totals_ref[...] = jnp.zeros_like(totals_ref)

    @pl.when(place_ref[0] != last)
    def _():
        copies = chunk_copies(chunk, density_ref, brick_ref, sem)
        for copy in copies:
            copy.start()
        row = lax.broadcasted_iota(jnp.int32, (16, 2 * lanes), 0)
        column = lax.broadcasted_iota(jnp.int32, (16, 2 * lanes), 1)
        pick = jnp.where(row == column // lanes, 1.0, 0.0).astype(jnp.bfloat16)

        def pair(v):
            return [brick_ref[v], brick_ref[half + v]]

        for k in range(half // chunk):
            copies[2 * k].wait()
            copies[2 * k + 1].wait()
            for v in range(k * chunk, (k + 1) * chunk, 4):
                left = jnp.concatenate(pair(v) + pair(v + 1), axis=0)
                right = jnp.concatenate(pair(v + 2) + pair(v + 3), axis=0)
                sums = lax.dot_general(
                    pick,
                    jnp.concatenate([left, right], axis=1),
                    (((1,), (1,)), ((), ())),
                    preferred_element_type=jnp.float32,
                )
                for j in range(4):
                    first = j % 2 * 2 * planes
                    totals_ref[v + j : v + j + 1] = sums[
                        j // 2 : j // 2 + 1, first : first + 2 * planes
                    ]


def brick_kernel(chunk, last, place_ref, density_ref, brick_in_ref, brick_ref, sem):
    @pl.when(place_ref[0] == last)
    def _():
        copies = chunk_copies(chunk, density_ref, brick_ref, sem)
        for copy in copies:
            copy.start()
        for copy in copies:
            copy.wait()


def local_kernel(
    rows,
    step_cells,
    light_parts,
    view_parts,
    place_ref,
    brick_ref,
    shade_ref,
    value_ref,
    still_ref,
):
    cells, planes, lanes = brick_ref.shape
    chunks = cells // step_cells
    before = lax.broadcasted_iota(jnp.int32, (lanes, lanes), 0)
    after = lax.broadcasted_iota(jnp.int32, (lanes, lanes), 1)
    depths = jnp.concatenate(
        [stacked(before < after, light_parts), stacked(before == after, view_parts)], axis=1
    )

    def fill(chunk, at):
        packed = brick_ref[pl.ds(chunk * step_cells, step_cells), at]
        flat = packed.reshape(step_cells * rows, lanes)
        depth = jnp.dot(
            jnp.concatenate([flat, flat], axis=1), depths, preferred_element_type=jnp.float32
        )
        return jnp.exp2(depth[:, :lanes]), jnp.exp2(depth[:, lanes:]), depth[:, lanes:]

    def use(chunk, at, buffer, state, first):
        through, *moments = state
        for j in range(step_cells):
            cell = chunk * step_cells + j
            lit, pass_on, value = (x[j * rows : (j + 1) * rows] for x in buffer)
            passed = through * pass_on
            weight = through - passed
            through = passed
            if first:
                weight = weight * (0.3 + lit)
                moments[0] = moments[0] + weight
            else:
                value_ref[cell, at] = value
                shade_ref[cell, at] = weight * lit
            for i in (1, 2, 3):
                weight = weight * value
                moments[i] = moments[i] + weight
        return through, *moments

    def run(first):
        blocks = [pl.ds(z, rows) for z in range(0, planes, rows)]
        for k, at in enumerate(blocks):
            zero = jnp.zeros((rows, lanes), jnp.float32)
            state = (jnp.ones((rows, lanes), jnp.float32), zero, zero, zero, zero)
            for chunk in range(chunks):
                state = use(chunk, at, fill(chunk, at), state, first)
            for i in range(5):
                still_ref[i, at] = state[i]

    @pl.when(place_ref[0] == 0)
    def _():
        run(True)

    @pl.when(place_ref[0] != 0)
    def _():
        run(False)


def lit_kernel(
    step_cells,
    light_scale,
    unit,
    picks,
    handed,
    take,
    place_ref,
    mine_ref,
    coef_ref,
    light_ref,
    still_ref,
    shade_ref,
    value_ref,
    *refs,
):
    outs, refs = refs[: len(picks)], refs[len(picks) :]
    passed, (reach_ref,) = refs[:-1], refs[-1:]
    cells, _, lanes = shade_ref.shape
    chunks = cells // step_cells
    chip, core = mine_ref[0] // 2, mine_ref[0] % 2

    def tile(place):
        if isinstance(place, int):
            return pl.ds(place, TILE)
        mask, side = place
        return pl.ds(pl.multiple_of((2 * (chip ^ mask) + (core ^ side)) * TILE, TILE), TILE)

    def rows(ref, pick, *index):
        if take and ref is not still_ref:
            return ref[*index]
        return jnp.concatenate([ref[*index, tile(place)] for place in pick], axis=0)

    def finish(out_ref, pick, moments):
        color = [
            sum(coef_ref[c : c + 1, i : i + 1] * unit**i * moments[i] for i in range(4))
            for c in range(3)
        ]
        for c, x in enumerate(color + [rows(still_ref, pick, 0)]):
            for k in range(2):
                out_ref[k, c] = x[k * TILE : (k + 1) * TILE]

    def parts(pick):
        reach = rows(reach_ref, pick)
        high = reach.astype(jnp.bfloat16)
        return high, (reach - high.astype(jnp.float32)).astype(jnp.bfloat16)

    def fill(chunk, both, pair, turns):
        first = chunk * step_cells // 2
        picked = [
            jnp.concatenate([jnp.where(pair == first + p, part, 0) for part in both], axis=1)
            for p in range(step_cells // 2)
        ]
        spread = jnp.dot(
            jnp.concatenate(picked, axis=0), turns, preferred_element_type=jnp.float32
        )
        return spread[:, :lanes], spread[:, lanes:]

    def use(chunk, pick, spread, state):
        m0, m1, m2, m3 = state
        for j in range(step_cells):
            cell = chunk * step_cells + j
            value = rows(value_ref, pick, cell)
            here = slice(j // 2 * 2 * TILE, (j // 2 + 1) * 2 * TILE)
            weight = rows(shade_ref, pick, cell) * spread[j % 2][here]
            m0 = m0 + weight
            weight = weight * value
            m1 = m1 + weight
            weight = weight * value
            m2 = m2 + weight
            weight = weight * value
            m3 = m3 + weight
        return m0, m1, m2, m3

    @pl.when(place_ref[0] == 0)
    def _():
        for pick, out_ref in zip(picks, outs):
            finish(out_ref, pick, [rows(still_ref, pick, 1 + i) for i in range(4)])

    @pl.when(place_ref[0] != 0)
    def _():
        pair = lax.broadcasted_iota(jnp.int32, (2 * TILE, cells), 1) // 2
        row = lax.broadcasted_iota(jnp.int32, (2 * cells, 2 * lanes), 0)
        column = lax.broadcasted_iota(jnp.int32, (2 * cells, 2 * lanes), 1)
        turns = jnp.where((row % 2 == 0) == (column < lanes), 1.0, 0.0).astype(jnp.bfloat16)
        if take:
            reach_ref[...] = light_ref[...]
        else:
            reach = jnp.exp2(light_ref[...] * light_scale).T
            half = reach.shape[0] // 2
            reach_ref[...] = jnp.concatenate([reach[:half], reach[half:]], axis=1)
        if handed is not None:
            passed[0][...] = rows(reach_ref, handed)
            for cell in range(cells):
                passed[1][cell] = rows(shade_ref, handed, cell)
                passed[2][cell] = rows(value_ref, handed, cell)
        for pick, out_ref in zip(picks, outs):
            both = parts(pick)
            state = (jnp.zeros((2 * TILE, lanes), jnp.float32),) * 4
            for chunk in range(chunks):
                state = use(chunk, pick, fill(chunk, both, pair, turns), state)
            m0 = state[0] + 0.3 * (1.0 - rows(still_ref, pick, 0))
            finish(
                out_ref,
                pick,
                [m0] + [state[i] + 0.3 * rows(still_ref, pick, 1 + i) for i in (1, 2, 3)],
            )


def over(pieces, order):
    total = 0.0
    for a, piece in enumerate(pieces):
        ahead = jnp.ones_like(piece[3])
        for b, other in enumerate(pieces):
            if a != b:
                ahead = ahead * jnp.where(order[b] < order[a], other[3], 1.0)
        total = total + piece[:3] * ahead[None]
    return total


def body(density, color_coef):
    cells, planes, lanes = density.shape
    light_count = lax.axis_size("light")
    view_count = lax.axis_size("view")
    light_scale = -2.0 / (lanes * light_count) * LOG2E
    view_parts = in_parts(-2.0 / (cells * view_count) * LOG2E)
    own_rows = planes // view_count
    chunk = 32
    step_cells = 16
    rows = 32
    lit_cells = 32
    whole = pl.BlockSpec(memory_space=VMEM)
    scalars = pl.BlockSpec(memory_space=pltpu.SMEM)

    place = lax.axis_index("light")
    where = place.astype(jnp.int32)[None]
    brick_shape = jax.ShapeDtypeStruct(density.shape, density.dtype)
    sem = pltpu.SemaphoreType.DMA((cells // chunk,))
    wide = pltpu.CompilerParams(vmem_limit_bytes=50 * 2**20 + 2**19)
    totals, brick = pl.pallas_call(
        functools.partial(totals_kernel, chunk, light_count - 1),
        name="totals_kernel",
        out_shape=[jax.ShapeDtypeStruct((cells // 2, 2 * planes), jnp.float32), brick_shape],
        in_specs=[scalars, pl.BlockSpec(memory_space=pltpu.HBM)],
        out_specs=[whole, whole],
        scratch_shapes=[sem],
        compiler_params=wide,
    )(where, density)

    arrived = [(mask, swapped(totals, "light", mask)) for mask in range(light_count - 1, 0, -1)]

    brick = pl.pallas_call(
        functools.partial(brick_kernel, chunk, light_count - 1),
        name="brick_kernel",
        out_shape=brick_shape,
        in_specs=[scalars, pl.BlockSpec(memory_space=pltpu.HBM), whole],
        out_specs=whole,
        input_output_aliases={2: 0},
        scratch_shapes=[sem],
        compiler_params=wide,
    )(where, density, brick)

    mine = lax.axis_index("view")
    core, chip = mine % 2, mine // 2
    chips = view_count // 2
    table = jax.ShapeDtypeStruct(density.shape, jnp.float32)
    shade, value, still = pl.pallas_call(
        functools.partial(local_kernel, rows, step_cells, in_parts(light_scale), view_parts),
        name="local_kernel",
        out_shape=[table, table, jax.ShapeDtypeStruct((5, planes, lanes), jnp.float32)],
        in_specs=[scalars, whole],
        out_specs=[whole] * 3,
        compiler_params=pltpu.CompilerParams(vmem_limit_bytes=8 * 2**20),
        cost_estimate=pl.CostEstimate(
            flops=20 * density.size, bytes_accessed=2**23, transcendentals=2 * density.size
        ),
    )(where, brick)

    upstream = jnp.zeros_like(totals)
    for mask, other in arrived:
        upstream = upstream + jnp.where(place ^ mask < place, other, 0.0)

    def lit(picks, light, shade, value, handed=None, take=False):
        reach = jax.ShapeDtypeStruct((2 * TILE if take else planes, cells), jnp.float32)
        table = jax.ShapeDtypeStruct((cells, 2 * TILE, lanes), jnp.float32)
        passed = []
        if handed is not None:
            passed = [jax.ShapeDtypeStruct((2 * TILE, cells), jnp.float32), table, table]
        return pl.pallas_call(
            functools.partial(
                lit_kernel, lit_cells, light_scale, 1.0 / sum(view_parts), picks, handed, take
            ),
            name="lit_kernel",
            out_shape=[jax.ShapeDtypeStruct((2, 4, TILE, lanes), jnp.float32)] * len(picks) + passed,
            in_specs=[scalars] * 2 + [whole] * 5,
            out_specs=[whole] * (len(picks) + len(passed)),
            scratch_shapes=[VMEM(reach.shape, reach.dtype)],
            compiler_params=pltpu.CompilerParams(vmem_limit_bytes=8 * 2**20),
        )(where, mine.astype(jnp.int32)[None], color_coef, light, still, shade, value)

    order = list(range(chips - 1, -1, -1))
    if own_rows == TILE and chips % 2 == 0:
        pairs = list(zip(order[::2], order[1::2]))
        give_picks = tuple(tuple((mask, 1) for mask in two) for two in pairs)
        keep_picks = tuple(tuple((mask, 0) for mask in two) for two in pairs)
        split = len(pairs)
        *first, reach, shade, value = lit(
            give_picks + keep_picks[:-1], upstream, shade, value, handed=keep_picks[-1]
        )
        give = jnp.concatenate(first[:split], axis=0)
        took = swapped(give, "view", 1)
        keep = jnp.concatenate(
            [*first[split:], *lit(keep_picks[-1:], reach, shade, value, take=True)], axis=0
        )
    else:
        picks = tuple((z, z + TILE) for z in range(0, planes, 2 * TILE))
        every = jnp.concatenate(lit(picks, upstream, shade, value), axis=0)
        every = jnp.swapaxes(every, 0, 1).reshape(4, chips, 2, own_rows, lanes)
        every = jnp.stack(
            [lax.dynamic_index_in_dim(every, chip ^ mask, 1, False) for mask in order]
        )
        give = lax.dynamic_index_in_dim(every, 1 - core, 2, False)
        keep = lax.dynamic_index_in_dim(every, core, 2, False)
        took = swapped(give, "view", 1)
    near = jnp.where(core == 0, keep, took)
    far = jnp.where(core == 0, took, keep)
    color = near[:, :3] + near[:, 3:] * far[:, :3]
    both = jnp.concatenate([color, near[:, 3:] * far[:, 3:]], axis=1)
    pieces = [swapped(both[k], "view", 2 * mask) for k, mask in enumerate(order[:-1])] + [both[-1]]
    return over(pieces, [chip ^ mask for mask in order])


def solution(mesh):
    placed = (P("view", None, "light"), P())
    return jax.shard_map(
        body, mesh=mesh, in_specs=placed, out_specs=P(None, "view", "light"), check_vma=False
    )
```
